32 devices in a mesh: seq: 8 (over z, y), head: 4 (over x, core).
Axes of the slice: x: 2, y: 2, z: 4, core: 2. Of those that a mesh axis runs over, the one named last changes fastest.
Arguments:
- tokens: bfloat16 [4096, 4096], P('seq'), may hold values from -6 to 6
- w_query: bfloat16 [4096, 4096], P(None, 'head'), may hold values from -0.09375 to 0.09375
- w_key: bfloat16 [4096, 4096], P(None, 'head'), may hold values from -0.09375 to 0.09375
- w_value: bfloat16 [4096, 4096], P(None, 'head'), may hold values from -0.09375 to 0.09375
- w_out: bfloat16 [4096, 4096], P('head'), may hold values from -0.125 to 0.125
- norm_gain: float32 [4096], P('head'), may hold values from 0.1 to 1.9
- level_weights: float32 [21, 32, 4096], P(None, 'head', 'seq'), may hold values from 0.00024414062 to 4, as said below
- prior_states: float32 [4, 32, 128, 128], P(None, 'head'), may hold values from -96 to 96
Outputs:
- layer_out: bfloat16 [4096, 4096], P('seq', 'head')
The draws below stay inside these ranges and needn't reach their ends.
Inputs may be any that keep to these rules, and one draw needn't show every extreme that they name: `level_weights`: positive.
All inputs are finite; a program needn't handle non-finite values.
Results may differ from the reference program's by a relative error of at most 0.022.
Values may be sent and summed in bfloat16 or wider, within the bound.
No kernel may reach another device: no remote copies, remote signals or barrier semaphores. Data moves between devices by JAX's collectives and lax.ppermute only.
A program may use at most 128 MiB of HBM per device.

```python
import math
import jax
import jax.numpy as jnp
from jax import lax

D = 4096
HEADS = 32
DH = 128
LEVELS = 21
PRIOR = 4
TOK_DEV = 512
TOKENS = 4096
N_HEAD = 4


def draw_level_weights(key, part):
    key = jax.random.fold_in(key, 11)
    shape = (LEVELS, HEADS, TOKENS)
    base = jnp.exp(jax.random.uniform(key, shape, jnp.float32, math.log(0.25), math.log(4.0)))
    level = jnp.arange(LEVELS, dtype=jnp.int32)
    factor = jnp.power(jnp.float32(0.5), (level // 2).astype(jnp.float32))
    return base * factor[:, None, None]


def draw_prior_states(key, part):
    key = jax.random.fold_in(key, 12)
    shape = (PRIOR, HEADS, DH, DH)
    base = jnp.clip(jax.random.normal(key, shape, jnp.float32), -3.0, 3.0)
    level = LEVELS - PRIOR + jnp.arange(PRIOR, dtype=jnp.int32)
    factor = jnp.power(jnp.float32(2.0), ((level - 1) // 2 - 4).astype(jnp.float32))
    return base * factor[:, None, None, None]


def strengthened(values, own_key, source, target, blocks, factor):
    def block_of(axis_at):
        return (jnp.arange(values.shape[axis_at]) // (values.shape[axis_at] // blocks)).reshape((-1,) + (1,) * (values.ndim - 1 - axis_at))

    first = jax.random.permutation(own_key, blocks)[block_of(target)]
    second = (block_of(target) + blocks // 2) % blocks
    return jnp.where((block_of(source) == first) | (block_of(source) == second), factor * values, values)


def level_of(key, shape, shards, smallest, top_value):
    def one(dim, parts):
        steps = jax.random.uniform(jax.random.fold_in(jax.random.fold_in(key, 6), dim), (parts,), jnp.float32, smallest / len(shards), top_value / len(shards))
        return jnp.repeat(jnp.exp(steps), shape[dim] // parts).reshape((-1,) + (1,) * (len(shape) - dim - 1))

    level = one(*shards[0])
    for cut in shards[1:]:
        level = level * one(*cut)
    return level


def centred(own_key, extent, width, bound, shards=(), kind=jnp.bfloat16):
    entries = width * jax.random.normal(own_key, extent, jnp.float32)
    if shards:
        entries = entries * level_of(own_key, extent, shards, -0.22, 0.18)
    return jnp.clip(entries, -bound, bound).astype(kind)


def bell_draw_with(stream_key, dims, spread, bound, cuts, heavy, kind=jnp.bfloat16):
    array = spread * jax.random.normal(stream_key, dims, jnp.float32)
    if cuts:
        array = array * level_of(stream_key, dims, cuts, -0.22, 0.18)
    return jnp.clip(strengthened(array, jax.random.fold_in(stream_key, 3), *heavy), -bound, bound).astype(kind)


def setup_inputs(seed: int = 0) -> dict:
    key_list = jax.random.split(jax.random.key(seed), 9)
    return {
        "tokens": centred(key_list[0], (TOKENS, D), 1.0, 6.0, ((0, 8),)),
        "w_query": centred(key_list[1], (D, HEADS * DH), D ** -0.5, 0.09375, ((1, 4),)),
        "w_key": centred(key_list[2], (D, HEADS * DH), D ** -0.5, 0.09375, ((1, 4),)),
        "w_value": centred(key_list[3], (D, HEADS * DH), D ** -0.5, 0.09375, ((1, 4),)),
        "w_out": bell_draw_with(key_list[4], (HEADS * DH, D), (HEADS * DH) ** -0.5, 0.125, ((0, 4),), (0, 1, 4, 2.0)),
        "norm_gain": jnp.clip(1.0 + 0.18 * jax.random.normal(key_list[5], (HEADS * DH,), jnp.float32), 0.1, 1.9),
        "level_weights": draw_level_weights(jax.random.fold_in(key_list[8], 71), 0),
        "prior_states": draw_prior_states(jax.random.fold_in(key_list[8], 71), 0),
    }


eps = 1e-06

def unit_heads(tokens, weight):
    raw = jnp.dot(tokens, weight, preferred_element_type=jnp.float32)
    raw = raw.reshape(raw.shape[0], HEADS, DH)
    return (raw * lax.rsqrt(lax.optimization_barrier(jnp.sum(raw * raw, axis=-1, keepdims=True)) + eps)).astype(jnp.bfloat16)

def block_attend(query_block, keys, values, lam, pos, cols, shift):
    scores = jnp.einsum('thd,shd->hts', query_block.astype(jnp.float32), keys.astype(jnp.float32))
    differ = jnp.bitwise_xor(pos[:, None], cols[None, :])
    level = jnp.zeros(differ.shape, jnp.int32)
    for bit in range(shift):
        level = level + (jnp.right_shift(differ, bit) > 0).astype(jnp.int32)
    weight = jnp.zeros(scores.shape, jnp.float32)
    for lv in range(shift + 1):
        weight = weight + jnp.where((level == lv)[None], lam[lv][:, :, None], jnp.float32(0.0))
    causal = cols[None, :] <= pos[:, None]
    mixing = jnp.where(causal[None], weight * scores, jnp.float32(0.0)).astype(jnp.bfloat16)
    return jnp.einsum('hts,shd->thd', mixing.astype(jnp.float32), values.astype(jnp.float32))

def reference(tokens, w_query, w_key, w_value, w_out, norm_gain, level_weights, prior_states):
    blocks = TOKENS // TOK_DEV
    shift = TOK_DEV.bit_length() - 1
    nbits = blocks.bit_length() - 1
    query = unit_heads(tokens, w_query)
    keys = unit_heads(tokens, w_key)
    values = jnp.dot(tokens, w_value, preferred_element_type=jnp.float32).astype(jnp.bfloat16).reshape(TOKENS, HEADS, DH)
    key_blocks = keys.reshape(blocks, TOK_DEV, HEADS, DH).astype(jnp.float32)
    value_blocks = values.reshape(blocks, TOK_DEV, HEADS, DH).astype(jnp.float32)
    states = jnp.einsum('nshd,nshe->nhde', key_blocks, value_blocks)
    lam_blocks = level_weights.reshape(LEVELS, HEADS, blocks, TOK_DEV).transpose(2, 0, 1, 3)
    peers = jnp.arange(blocks, dtype=jnp.int32)
    cols = jnp.arange(TOK_DEV, dtype=jnp.int32)
    picks = [1 + shift + bit for bit in range(nbits)] + [LEVELS - PRIOR + p for p in range(PRIOR)]

    def one_block(index):
        start = (index * TOK_DEV).astype(jnp.int32)
        q_here = lax.dynamic_slice_in_dim(query, start, TOK_DEV, 0)
        k_here = lax.dynamic_slice_in_dim(keys, start, TOK_DEV, 0)
        v_here = lax.dynamic_slice_in_dim(values, start, TOK_DEV, 0)
        lam = lam_blocks[index]
        near = block_attend(q_here, k_here, v_here, lam, cols, cols, shift)
        level_states = []
        for bit in range(nbits):
            chosen = (index >> bit & 1 == 1) & (peers >> bit + 1 == index >> bit + 1) & (peers >> bit & 1 == 0)
            level_states.append(jnp.einsum('n,nhde->hde', chosen.astype(jnp.float32), states, precision=lax.Precision.HIGHEST))
        stacked = jnp.stack(level_states + [prior_states[p] for p in range(PRIOR)])
        lam_far = jnp.stack([lam[row] for row in picks])
        weighted = lam_far.transpose(0, 2, 1)[..., None] * q_here.astype(jnp.float32)[None]
        far = jnp.einsum('lthd,lhde->the', weighted, stacked, precision=lax.Precision.HIGHEST)
        return near + far
    mixed = lax.map(one_block, jnp.arange(blocks, dtype=jnp.int32)).reshape(TOKENS, HEADS, DH)
    scale = lax.rsqrt(lax.optimization_barrier(jnp.mean(mixed * mixed, axis=-1, keepdims=True)) + eps)
    normed = (mixed * scale * norm_gain.reshape(HEADS, DH)).astype(jnp.bfloat16).reshape(TOKENS, HEADS * DH)
    group = HEADS * DH // N_HEAD

    def add_group(total, index):
        start = (index * group).astype(jnp.int32)
        piece = lax.dynamic_slice_in_dim(normed, start, group, 1)
        rows = lax.dynamic_slice_in_dim(w_out, start, group, 0)
        term = jnp.dot(piece, rows, preferred_element_type=jnp.float32).astype(jnp.bfloat16)
        term = lax.optimization_barrier(term)
        return (total + term.astype(jnp.float32), None)
    total, _ = lax.scan(add_group, jnp.zeros((TOKENS, D), jnp.float32), jnp.arange(N_HEAD, dtype=jnp.int32))
    return total.astype(jnp.bfloat16)
```

```python
import functools

import jax
import jax.numpy as jnp
from jax import lax
from jax.experimental import pallas as pl
from jax.experimental.pallas import tpu as pltpu
from jax.sharding import PartitionSpec as P

eps = 1e-06
TILE = 128
MIB = 1024 * 1024
f32, bf16 = jnp.float32, jnp.bfloat16
HBM = pl.BlockSpec(memory_space=pltpu.HBM)
VMEM = pl.BlockSpec(memory_space=pltpu.VMEM)
SMEM = pl.BlockSpec(memory_space=pltpu.SMEM)
ANY = pl.BlockSpec(memory_space=pl.ANY)


def mm(a, b):
    return jnp.dot(a, b, preferred_element_type=f32)


def params(mib):
    return pltpu.CompilerParams(vmem_limit_bytes=mib * MIB)


def cost(flops, size):
    return pl.CostEstimate(flops=int(flops) // 100, bytes_accessed=int(size) // 100, transcendentals=0)


FAR_APART = pl.CostEstimate(flops=4 * 10**10, bytes_accessed=10**8, transcendentals=0)


def in_hbm(x):
    return pltpu.with_memory_space_constraint(x, pltpu.HBM)


def starts(copies):
    for copy in copies:
        copy.start()


def keys_values_body(
    width, x_hbm, wk_hbm, wv_hbm, wq_hbm, x, wq, k_ref, vt_ref, keep_ref, give_ref, wk, wv, k_acc, v_acc, s, sem
):
    rows, depth = x.shape
    size = wk.shape[1]
    cuts = sem.shape[1]
    cut = depth // cuts
    at = [pl.ds(c * cut, cut) for c in range(cuts)]
    x_in = [pltpu.make_async_copy(x_hbm.at[:, a], x.at[:, a], sem.at[0, c]) for c, a in enumerate(at)]
    v_in = [pltpu.make_async_copy(wv_hbm.at[a], wv.at[a], sem.at[1, c]) for c, a in enumerate(at)]
    k_in = [pltpu.make_async_copy(wk_hbm.at[a], wk.at[a], sem.at[2, c]) for c, a in enumerate(at)]
    q_in = [pltpu.make_async_copy(wq_hbm.at[a], wq.at[a], sem.at[3, c]) for c, a in enumerate(at)]
    for c in range(cuts):
        starts((x_in[c], v_in[c]))
    starts(k_in)
    starts(q_in)
    heads = size // width
    half = heads // 2
    own = [slice(h * width, (h + 1) * width) for h in range(heads)]
    for c, a in enumerate(at):
        x_in[c].wait()
        v_in[c].wait()
        term = mm(x[:, a], wv[a, :])
        v_acc[...] = term if c == 0 else v_acc[...] + term
    for c, a in enumerate(at):
        k_in[c].wait()
        term = mm(x[:, a], wk[a, :])
        k_acc[...] = term if c == 0 else k_acc[...] + term
        for h in range(c * heads // cuts, (c + 1) * heads // cuts):
            vt_ref[own[h], :] = v_acc[:, own[h]].T.astype(bf16)
    for h in range(heads):
        raw = k_acc[:, own[h]]
        key = (raw * lax.rsqrt(jnp.sum(raw * raw, axis=-1, keepdims=True) + eps)).astype(bf16)
        k_ref[:, own[h]] = key
        s[h] = mm(vt_ref[own[h], :], key).astype(bf16)
    first = (lax.axis_index("seq") & 1) * half
    for h in range(half):
        keep_ref[h] = s[first + h]
        give_ref[h] = s[half - first + h]
    for copy in q_in:
        copy.wait()


def keys_values(tokens, w_key, w_value, w_query, width):
    rows, depth = tokens.shape
    size = w_key.shape[1]
    heads = size // width
    cuts = 8
    part = pltpu.VMEM((heads // 2, width, width), bf16)
    return pl.pallas_call(
        functools.partial(keys_values_body, width),
        in_specs=[HBM] * 4,
        out_specs=[VMEM] * 6,
        out_shape=[
            pltpu.VMEM((rows, depth), bf16),
            pltpu.VMEM((depth, size), bf16),
            pltpu.VMEM((rows, size), bf16),
            pltpu.VMEM((size, rows), bf16),
            part,
            part,
        ],
        scratch_shapes=[
            pltpu.VMEM((depth, size), bf16),
            pltpu.VMEM((depth, size), bf16),
            pltpu.VMEM((rows, size), f32),
            pltpu.VMEM((rows, size), f32),
            pltpu.VMEM((heads, width, width), bf16),
            pltpu.SemaphoreType.DMA((4, cuts)),
        ],
        compiler_params=params(30),
        cost_estimate=cost(4 * rows * depth * size, 2 * (rows * depth + 2 * depth * size)),
        name="keys_values",
    )(in_hbm(tokens), in_hbm(w_key), in_hbm(w_value), in_hbm(w_query))


def attend(qt, k, vt, lam, prior):
    width, rows = qt.shape
    shift = rows.bit_length() - 1
    low = TILE.bit_length() - 1
    levels, priors = lam.shape[0], len(prior)
    product = mm(jnp.concatenate([p.astype(bf16).T for p in prior], axis=0), qt)
    total = lam[levels - priors : levels - priors + 1] * product[:width]
    for p in range(1, priors):
        lv = levels - priors + p
        total = total + lam[lv : lv + 1] * product[p * width : (p + 1) * width]
    t_at = lax.broadcasted_iota(jnp.int32, (8, rows), 1) & 7
    s_at = lax.broadcasted_iota(jnp.int32, (8, rows), 0)
    near = jnp.zeros((8, rows), f32)
    for lv in range(4):
        picked = (t_at ^ s_at) >= (1 << lv >> 1)
        near = jnp.where(picked, lam[lv : lv + 1], near)
    near = jnp.where(s_at <= t_at, near, 0.0)
    groups = TILE // 8
    t_group = (lax.broadcasted_iota(jnp.int32, (groups, rows), 1) & (TILE - 1)) >> 3
    s_group = lax.broadcasted_iota(jnp.int32, (groups, rows), 0)
    wide = jnp.zeros((groups, rows), f32)
    for lv in range(4, low + 1):
        picked = (t_group ^ s_group) >= (1 << (lv - 4))
        wide = jnp.where(picked, lam[lv : lv + 1], wide)
    wide = jnp.where(s_group < t_group, wide, 0.0)
    lane_group = (lax.broadcasted_iota(jnp.int32, (8, TILE), 1)) >> 3
    pieces = []
    for i in range(rows // TILE):
        here = slice(i * TILE, (i + 1) * TILE)
        scores = mm(k[here], qt[:, here])
        mixing = []
        for g in range(groups):
            weight = jnp.where(lane_group == g, near[:, here], wide[g : g + 1, here])
            mixing.append(weight * scores[g * 8 : g * 8 + 8])
        mixing = jnp.concatenate(mixing, axis=0).astype(bf16)
        pieces.append(total[:, here] + mm(vt[:, here], mixing))
    for bit in range(low, shift):
        half = 1 << bit
        for start in range(half, rows, 2 * half):
            past = slice(start - half, start)
            here = slice(start, start + half)
            state = mm(vt[:, past], k[past]).astype(bf16)
            found = lam[1 + bit : 2 + bit, here] * mm(state, qt[:, here])
            for n in range(half // TILE):
                i = start // TILE + n
                pieces[i] = pieces[i] + found[:, n * TILE : (n + 1) * TILE]
    return pieces


def attend_into(acc_ref, at, head, h, width, qt, k_ref, vt_ref, lam_ref, prior_ref):
    own = slice(h * width, (h + 1) * width)
    prior = [prior_ref[p, h] for p in range(prior_ref.shape[0])]
    pieces = attend(qt, k_ref[:, own], vt_ref[own, :], lam_ref[:, head, :], prior)
    for i, piece in enumerate(pieces):
        acc_ref[i, at * width : (at + 1) * width, :] = piece


def whole(qt_ref, at):
    return jnp.concatenate([qt_ref[i, at, :] for i in range(qt_ref.shape[0])], axis=1)


def queries_body(width, part, flip, count, x, wq, after, w_hbm, *refs):
    sources, qt_ref, w_ref, targets, sem = refs[:count], refs[count], refs[count + 1], refs[count + 2 : -1], refs[-1]
    copies = [pltpu.make_async_copy(a, b, sem.at[n]) for n, (a, b) in enumerate(zip(sources, targets))]
    chips, _, columns = w_ref.shape
    group = lax.axis_index("head") ^ flip
    for d in range(chips):
        base = pl.multiple_of(lax.rem(group + 2 * d, 2 * chips) * columns, 128)
        copies.append(pltpu.make_async_copy(w_hbm.at[:, pl.ds(base, columns)], w_ref.at[d], sem.at[count + d]))
    starts(copies)
    rows = x.shape[0]
    size = qt_ref.shape[1]
    step = min(256, size)
    for first in range(0, size, step):
        raw_step = mm(x[...], wq[:, part * size + first : part * size + first + step])
        for h in range(step // width):
            raw = raw_step[:, h * width : (h + 1) * width].T
            qt = (raw * lax.rsqrt(jnp.sum(raw * raw, axis=0, keepdims=True) + eps)).astype(bf16)
            own = slice(first + h * width, first + (h + 1) * width)
            for i in range(rows // TILE):
                qt_ref[i, own, :] = qt[:, i * TILE : (i + 1) * TILE]
    for copy in copies:
        copy.wait()


def queries(tokens, w_query, after, w_out, flip, chips, width, part, fetch=()):
    rows, depth = tokens.shape
    size = w_query.shape[1] // 2
    columns = w_out.shape[1] // (2 * chips)
    return pl.pallas_call(
        functools.partial(queries_body, width, part, flip, len(fetch)),
        in_specs=[VMEM, VMEM, ANY, HBM] + [HBM] * len(fetch),
        out_specs=[VMEM] * (2 + len(fetch)),
        out_shape=[pltpu.VMEM((rows // TILE, size, TILE), bf16), pltpu.VMEM((chips, w_out.shape[0], columns), bf16)]
        + [pltpu.VMEM(a.shape, a.dtype) for a in fetch],
        scratch_shapes=[pltpu.SemaphoreType.DMA((len(fetch) + chips,))],
        compiler_params=params(16),
        cost_estimate=cost(2 * rows * depth * size, 2 * (rows * depth + depth * size)),
        name="queries",
    )(tokens, w_query, after, in_hbm(w_out), *[in_hbm(a) for a in fetch])


def attention_body(width, halves, k_ref, vt_ref, lam_ref, prior_ref, after, *refs):
    qt_refs, acc_ref = refs[:halves], refs[halves]
    heads = prior_ref.shape[1]
    per = heads // halves
    for h in range(heads):
        qt = whole(qt_refs[h // per], slice(h % per * width, (h % per + 1) * width))
        attend_into(acc_ref, h, h, h, width, qt, k_ref, vt_ref, lam_ref, prior_ref)


def attention(queries_t, keys, values_t, level_weights, prior_states, after, width):
    tiles, _, take = queries_t[0].shape
    total = keys.shape[1]
    return pl.pallas_call(
        functools.partial(attention_body, width, len(queries_t)),
        in_specs=[VMEM] * 4 + [ANY] + [VMEM] * len(queries_t),
        out_specs=VMEM,
        out_shape=pltpu.VMEM((tiles, total, take), f32),
        compiler_params=params(16),
        cost_estimate=cost(12 * tiles * take * width * total, 8 * tiles * take * total),
        name="attention",
    )(keys, values_t, level_weights, prior_states, after, *queries_t)


def far_body(width, first_level, halves, nbits, first, number, after, *refs):
    qt_refs = refs[:halves]
    acc_ref = refs[halves]
    state_refs = refs[halves + 1 : halves + 1 + 2 * nbits]
    lam_ref, gain_ref, out_ref = refs[halves + 1 + 2 * nbits :]
    heads = lam_ref.shape[1]
    half = heads // 2
    per = heads // halves
    mine = lax.axis_index("seq")
    odd = (mine & 1) > 0
    for head in range(heads):
        own = slice(head * width, (head + 1) * width)
        states = []
        for j in range(nbits):
            kept, swapped = state_refs[2 * j][head % half], state_refs[2 * j + 1][head % half]
            if j == 0:
                states.append(kept if head >= half else swapped)
            else:
                states.append(jnp.where(odd, kept, swapped) if head >= half else jnp.where(odd, swapped, kept))
        states = jnp.concatenate(states, axis=0)
        for i in range(number):
            tile = first + i
            qt = qt_refs[head // per][tile, head % per * width : (head % per + 1) * width, :]
            product = mm(states, qt)
            total = acc_ref[tile, own, :]
            for j in range(nbits):
                lam = lam_ref[first_level + j, head : head + 1, tile * TILE : (tile + 1) * TILE]
                lam = jnp.where(((mine >> j) & 1) > 0, lam, 0.0)
                total = total + lam * product[j * width : (j + 1) * width]
            scale = lax.rsqrt(jnp.mean(total * total, axis=0, keepdims=True) + eps)
            out_ref[i * TILE : (i + 1) * TILE, own] = ((total * scale).T * gain_ref[:, own]).astype(bf16)


def far_part(after, queries_t, acc, states, level_weights, gain, width, first, number):
    levels, heads, rows = level_weights.shape
    total = heads * width
    halves = len(queries_t)
    return pl.pallas_call(
        functools.partial(far_body, width, rows.bit_length(), halves, len(states) // 2, first, number),
        in_specs=[ANY] + [VMEM] * (halves + 3 + len(states)),
        out_specs=VMEM,
        out_shape=pltpu.VMEM((number * TILE, total), bf16),
        compiler_params=params(16),
        cost_estimate=cost(8 * rows * width * total, 8 * rows * total),
        name="far_part",
    )(after, *queries_t, acc, *states, level_weights, gain)


def project_body(d, count, after, w, w_twin, *refs):
    mine, twins, out_ref = refs[:count], refs[count : 2 * count], refs[2 * count]
    columns = w.shape[2]
    step = min(256, columns)
    for first in range(0, columns, step):
        here = slice(first, first + step)
        row = 0
        for a, b in zip(mine, twins):
            take = a.shape[0]
            total = mm(a[...], w[d, :, here]) + mm(b[...], w_twin[d, :, here])
            out_ref[row : row + take, here] = total.astype(out_ref.dtype)
            row += take


def project(after, w, w_twin, mine, twins, kind, d, estimate=None):
    _, depth, columns = w.shape
    take = sum(a.shape[0] for a in mine)
    return pl.pallas_call(
        functools.partial(project_body, d, len(mine)),
        in_specs=[ANY, VMEM, VMEM] + [VMEM] * (2 * len(mine)),
        out_specs=VMEM,
        out_shape=pltpu.VMEM((take, columns), kind),
        compiler_params=params(16),
        cost_estimate=estimate or cost(4 * take * depth * columns, 4 * depth * columns),
        name="project",
    )(after, w, w_twin, *mine, *twins)


def finish_body(count, out_in, own_ref, *refs):
    out_ref = refs[-1]
    total = own_ref[...]
    for ref in refs[:count]:
        total = total + ref[...].astype(f32)
    out_ref[...] = total.astype(bf16)


def finish(out, own, terms, first):
    rows, columns = own.shape
    place = lambda i: (first // TILE + i, 0)
    return pl.pallas_call(
        functools.partial(finish_body, len(terms)),
        grid=(terms[0].shape[0] // TILE,),
        in_specs=[ANY, pl.BlockSpec((TILE, columns), place)]
        + [pl.BlockSpec((TILE, columns), lambda i: (i, 0))] * len(terms),
        out_specs=pl.BlockSpec((TILE, columns), place),
        out_shape=jax.ShapeDtypeStruct((rows, columns), bf16),
        input_output_aliases={0: 0} if first else {},
        compiler_params=params(16),
        cost_estimate=FAR_APART,
        name="finish",
    )(out, own, *terms)


def per_device(tokens, w_query, w_key, w_value, w_out, norm_gain, level_weights, prior_states):
    levels, heads, rows = level_weights.shape
    width = prior_states.shape[-1]
    count = lax.axis_size("seq")
    nbits = count.bit_length() - 1
    groups = lax.axis_size("head")
    chips = groups // 2
    twin = [(i, i ^ 1) for i in range(groups)]
    gain = norm_gain.reshape(1, heads * width)

    def send(state, j):
        return lax.ppermute(state, "seq", [(r, r ^ (1 << j)) for r in range(count)])

    def merge(state, got):
        return (state.astype(f32) + got.astype(f32)).astype(bf16)

    def not_before(value, done):
        return lax.optimization_barrier((value, done))[0]

    tokens, w_query, keys, values_t, keep, give = keys_values(tokens, w_key, w_value, w_query, width)
    got = send(give, 0)
    q_a, w_give, level_weights, prior_states = queries(
        tokens, w_query, keep, w_out, 1, chips, width, 0, (level_weights, prior_states)
    )
    got = not_before(got, q_a)
    running = merge(keep, got)
    states = [got]
    for j in range(1, nbits):
        got = send(running, j)
        if j == 1:
            w_twin = lax.ppermute(not_before(w_give, running), "head", twin)
            states.append(send(not_before(keep, running), 0))
            done, w = queries(tokens, w_query, running, w_out, 0, chips, width, 1)
            queries_t = [q_a, done]
        elif j == nbits - 1:
            done = acc = attention(queries_t, keys, values_t, level_weights, prior_states, running, width)
        got = not_before(got, done)
        if j < nbits - 1:
            running = merge(running, got)
        states += [got, send(got, 0)]

    first = far_part(acc, queries_t, acc, states, level_weights, gain, width, 0, 1)
    first_twin = lax.ppermute(first, "head", twin)
    rest = far_part(first, queries_t, acc, states, level_weights, gain, width, 1, rows // TILE - 1)
    rest_twin = lax.ppermute(rest, "head", twin)
    after = rest
    received = []
    for mine, other, estimate in ((first, first_twin, FAR_APART), (rest, rest_twin, None)):
        terms = []
        for d in range(1, chips):
            after = project(after, w, w_twin, [mine], [other], bf16, d, estimate)
            terms.append(lax.ppermute(after, "head", [(i, (i + 2 * d) % groups) for i in range(groups)]))
        received.append(terms)
    own = project(after, w, w_twin, [first, rest], [first_twin, rest_twin], f32, 0)
    out = finish(gain, own, received[0], 0)
    return finish(out, own, received[1], TILE)


def solution(mesh):
    placed = (
        P("seq", None),
        P(None, "head"),
        P(None, "head"),
        P(None, "head"),
        P("head", None),
        P("head"),
        P(None, "head", "seq"),
        P(None, "head", None, None),
    )
    return jax.shard_map(
        per_device, mesh=mesh, in_specs=placed, out_specs=P("seq", "head"), check_vma=False
    )
```

```python
import functools

import jax
import jax.numpy as jnp
from jax import lax
from jax.experimental import pallas as pl
from jax.experimental.pallas import tpu as pltpu
from jax.sharding import PartitionSpec as P

eps = 1e-06
TILE = 128
MIB = 1024 * 1024
f32, bf16 = jnp.float32, jnp.bfloat16
HBM = pl.BlockSpec(memory_space=pltpu.HBM)
VMEM = pl.BlockSpec(memory_space=pltpu.VMEM)
SMEM = pl.BlockSpec(memory_space=pltpu.SMEM)
ANY = pl.BlockSpec(memory_space=pl.ANY)


def mm(a, b):
    return jnp.dot(a, b, preferred_element_type=f32)


def params(mib):
    return pltpu.CompilerParams(vmem_limit_bytes=mib * MIB)


def cost(flops, size):
    return pl.CostEstimate(flops=int(flops) // 100, bytes_accessed=int(size) // 100, transcendentals=0)


FAR_APART = pl.CostEstimate(flops=4 * 10**10, bytes_accessed=10**8, transcendentals=0)


def in_hbm(x):
    return pltpu.with_memory_space_constraint(x, pltpu.HBM)


def starts(copies):
    for copy in copies:
        copy.start()


def keys_values_body(
    width, x_hbm, wk_hbm, wv_hbm, wq_hbm, x, wq, k_ref, vt_ref, keep_ref, give_ref, wk, wv, k_acc, v_acc, s, sem
):
    rows, depth = x.shape
    size = wk.shape[1]
    cuts = sem.shape[1]
    cut = depth // cuts
    at = [pl.ds(c * cut, cut) for c in range(cuts)]
    x_in = [pltpu.make_async_copy(x_hbm.at[:, a], x.at[:, a], sem.at[0, c]) for c, a in enumerate(at)]
    v_in = [pltpu.make_async_copy(wv_hbm.at[a], wv.at[a], sem.at[1, c]) for c, a in enumerate(at)]
    k_in = [pltpu.make_async_copy(wk_hbm.at[a], wk.at[a], sem.at[2, c]) for c, a in enumerate(at)]
    first_half = pl.ds(0, size // 2)
    q_in = [pltpu.make_async_copy(wq_hbm.at[a, first_half], wq.at[a], sem.at[3, c]) for c, a in enumerate(at)]
    for c in range(cuts):
        starts((x_in[c], v_in[c]))
    starts(k_in)
    starts(q_in)
    heads = size // width
    half = heads // 2
    own = [slice(h * width, (h + 1) * width) for h in range(heads)]
    for c, a in enumerate(at):
        x_in[c].wait()
        v_in[c].wait()
        term = mm(x[:, a], wv[a, :])
        v_acc[...] = term if c == 0 else v_acc[...] + term
    for c, a in enumerate(at):
        k_in[c].wait()
        term = mm(x[:, a], wk[a, :])
        k_acc[...] = term if c == 0 else k_acc[...] + term
        for h in range(c * heads // cuts, (c + 1) * heads // cuts):
            vt_ref[own[h], :] = v_acc[:, own[h]].T.astype(bf16)
    for h in range(heads):
        raw = k_acc[:, own[h]]
        key = (raw * lax.rsqrt(jnp.sum(raw * raw, axis=-1, keepdims=True) + eps)).astype(bf16)
        k_ref[:, own[h]] = key
        s[h] = mm(vt_ref[own[h], :], key).astype(bf16)
    first = (lax.axis_index("seq") & 1) * half
    for h in range(half):
        keep_ref[h] = s[first + h]
        give_ref[h] = s[half - first + h]
    for copy in q_in:
        copy.wait()


def keys_values(tokens, w_key, w_value, w_query, width):
    rows, depth = tokens.shape
    size = w_key.shape[1]
    heads = size // width
    cuts = 8
    part = pltpu.VMEM((heads // 2, width, width), bf16)
    return pl.pallas_call(
        functools.partial(keys_values_body, width),
        in_specs=[HBM] * 4,
        out_specs=[VMEM] * 6,
        out_shape=[
            pltpu.VMEM((rows, depth), bf16),
            pltpu.VMEM((depth, size // 2), bf16),
            pltpu.VMEM((rows, size), bf16),
            pltpu.VMEM((size, rows), bf16),
            part,
            part,
        ],
        scratch_shapes=[
            pltpu.VMEM((depth, size), bf16),
            pltpu.VMEM((depth, size), bf16),
            pltpu.VMEM((rows, size), f32),
            pltpu.VMEM((rows, size), f32),
            pltpu.VMEM((heads, width, width), bf16),
            pltpu.SemaphoreType.DMA((4, cuts)),
        ],
        compiler_params=params(30),
        cost_estimate=cost(4 * rows * depth * size, 2 * (rows * depth + 2 * depth * size)),
        name="keys_values",
    )(in_hbm(tokens), in_hbm(w_key), in_hbm(w_value), in_hbm(w_query))


def attend(qt, k, vt, lam, prior):
    width, rows = qt.shape
    shift = rows.bit_length() - 1
    low = TILE.bit_length() - 1
    levels, priors = lam.shape[0], len(prior)
    product = mm(jnp.concatenate([p.astype(bf16).T for p in prior], axis=0), qt)
    total = lam[levels - priors : levels - priors + 1] * product[:width]
    for p in range(1, priors):
        lv = levels - priors + p
        total = total + lam[lv : lv + 1] * product[p * width : (p + 1) * width]
    t_at = lax.broadcasted_iota(jnp.int32, (8, rows), 1) & 7
    s_at = lax.broadcasted_iota(jnp.int32, (8, rows), 0)
    near = jnp.zeros((8, rows), f32)
    for lv in range(4):
        picked = (t_at ^ s_at) >= (1 << lv >> 1)
        near = jnp.where(picked, lam[lv : lv + 1], near)
    near = jnp.where(s_at <= t_at, near, 0.0)
    groups = TILE // 8
    t_group = (lax.broadcasted_iota(jnp.int32, (groups, rows), 1) & (TILE - 1)) >> 3
    s_group = lax.broadcasted_iota(jnp.int32, (groups, rows), 0)
    wide = jnp.zeros((groups, rows), f32)
    for lv in range(4, low + 1):
        picked = (t_group ^ s_group) >= (1 << (lv - 4))
        wide = jnp.where(picked, lam[lv : lv + 1], wide)
    wide = jnp.where(s_group < t_group, wide, 0.0)
    lane_group = (lax.broadcasted_iota(jnp.int32, (8, TILE), 1)) >> 3
    pieces = []
    for i in range(rows // TILE):
        here = slice(i * TILE, (i + 1) * TILE)
        scores = mm(k[here], qt[:, here])
        mixing = []
        for g in range(groups):
            weight = jnp.where(lane_group == g, near[:, here], wide[g : g + 1, here])
            mixing.append(weight * scores[g * 8 : g * 8 + 8])
        mixing = jnp.concatenate(mixing, axis=0).astype(bf16)
        pieces.append(total[:, here] + mm(vt[:, here], mixing))
    for bit in range(low, shift):
        half = 1 << bit
        for start in range(half, rows, 2 * half):
            past = slice(start - half, start)
            here = slice(start, start + half)
            state = mm(vt[:, past], k[past]).astype(bf16)
            found = lam[1 + bit : 2 + bit, here] * mm(state, qt[:, here])
            for n in range(half // TILE):
                i = start // TILE + n
                pieces[i] = pieces[i] + found[:, n * TILE : (n + 1) * TILE]
    return pieces


def whole(qt_ref, at):
    return jnp.concatenate([qt_ref[i, at, :] for i in range(qt_ref.shape[0])], axis=1)


def finished(raw):
    raw = raw.T
    return (raw * lax.rsqrt(jnp.sum(raw * raw, axis=0, keepdims=True) + eps)).astype(bf16)


def leave_tiles(ref, at, qt):
    for i in range(ref.shape[0]):
        ref[i, at, :] = qt[:, i * TILE : (i + 1) * TILE]


def row_copies(source, first, target, sem, at, pieces):
    cut = target.shape[0] // pieces
    return [
        pltpu.make_async_copy(source.at[pl.ds(first + c * cut, cut)], target.at[pl.ds(c * cut, cut)], sem.at[at + c])
        for c in range(pieces)
    ]


def query_product(x, wq, raw_ref, meanwhile):
    rows, depth = x.shape
    cuts = 8
    cut = depth // cuts
    for c in range(cuts):
        a = slice(c * cut, (c + 1) * cut)
        term = mm(x[:, a], wq[a, :])
        raw_ref[...] = term if c == 0 else raw_ref[...] + term
        meanwhile(c, cuts)


def queries_first_body(x, wq, wq_hbm, lam_hbm, prior_hbm, after, raw_ref, wq_next, lam, prior, sem):
    depth, size = wq.shape
    cut = depth // 8
    copies = [pltpu.make_async_copy(lam_hbm, lam, sem.at[0])]
    for c in range(8):
        a = pl.ds(c * cut, cut)
        copies.append(pltpu.make_async_copy(wq_hbm.at[a, pl.ds(size, size)], wq_next.at[a], sem.at[1 + c]))
    for p in range(prior.shape[0]):
        copies.append(pltpu.make_async_copy(prior_hbm.at[p], prior.at[p], sem.at[9 + p]))
    starts(copies)
    query_product(x, wq, raw_ref, lambda c, cuts: None)
    for copy in copies:
        copy.wait()


def queries_first(tokens, half_query, w_query, level_weights, prior_states, after):
    rows, depth = tokens.shape
    size = half_query.shape[1]
    return pl.pallas_call(
        queries_first_body,
        in_specs=[VMEM, VMEM, HBM, HBM, HBM, ANY],
        out_specs=[VMEM] * 4,
        out_shape=[
            pltpu.VMEM((rows, size), f32),
            pltpu.VMEM(half_query.shape, bf16),
            pltpu.VMEM(level_weights.shape, f32),
            pltpu.VMEM(prior_states.shape, f32),
        ],
        scratch_shapes=[pltpu.SemaphoreType.DMA((9 + prior_states.shape[0],))],
        compiler_params=params(16),
        cost_estimate=cost(2 * rows * depth * size, 2 * (rows * depth + depth * size)),
        name="queries_first",
    )(tokens, half_query, in_hbm(w_query), in_hbm(level_weights), in_hbm(prior_states), after)


def queries_second_body(width, x, wq, raw_old, w_hbm, after, qt_ref, raw_ref, w_ref, sem):
    copies = row_copies(w_hbm, 0, w_ref, sem, 0, 8)
    starts(copies)
    heads = raw_old.shape[1] // width

    def meanwhile(c, cuts):
        for h in range(c * heads // cuts, (c + 1) * heads // cuts):
            own = slice(h * width, (h + 1) * width)
            leave_tiles(qt_ref, own, finished(raw_old[:, own]))

    query_product(x, wq, raw_ref, meanwhile)
    for copy in copies:
        copy.wait()


def queries_second(tokens, half_query, raw_old, w_out, after, width):
    rows, depth = tokens.shape
    size = half_query.shape[1]
    return pl.pallas_call(
        functools.partial(queries_second_body, width),
        in_specs=[VMEM, VMEM, VMEM, HBM, ANY],
        out_specs=[VMEM] * 3,
        out_shape=[
            pltpu.VMEM((rows // TILE, size, TILE), bf16),
            pltpu.VMEM((rows, size), f32),
            pltpu.VMEM((w_out.shape[0] // 2, w_out.shape[1]), bf16),
        ],
        scratch_shapes=[pltpu.SemaphoreType.DMA((8,))],
        compiler_params=params(16),
        cost_estimate=cost(2 * rows * depth * size, 2 * (rows * depth + depth * size)),
        name="queries_second",
    )(tokens, half_query, raw_old, in_hbm(w_out), after)


def attention_body(width, lam_ref, prior_ref, w_hbm, after, qt_old, raw, k_ref, vt_ref, acc_ref, qt_ref, w_ref, sem):
    copies = row_copies(w_hbm, w_ref.shape[0], w_ref, sem, 0, 8)
    starts(copies)
    heads = prior_ref.shape[1]
    per = heads // 2
    for h in range(heads):
        own = slice(h % per * width, (h % per + 1) * width)
        every = slice(h * width, (h + 1) * width)
        if h < per:
            qt = whole(qt_old, own)
        else:
            qt = finished(raw[:, own])
            leave_tiles(qt_ref, own, qt)
        prior = [prior_ref[p, h] for p in range(prior_ref.shape[0])]
        pieces = attend(qt, k_ref[:, every], vt_ref[every, :], lam_ref[:, h, :], prior)
        for i, piece in enumerate(pieces):
            acc_ref[i, every, :] = piece
    for copy in copies:
        copy.wait()


def attention(qt_old, raw, keys, values_t, level_weights, prior_states, w_out, after, width):
    tiles, size, take = qt_old.shape
    return pl.pallas_call(
        functools.partial(attention_body, width),
        in_specs=[VMEM] * 2 + [HBM, ANY] + [VMEM] * 4,
        out_specs=[VMEM] * 3,
        out_shape=[
            pltpu.VMEM((tiles, 2 * size, take), f32),
            pltpu.VMEM(qt_old.shape, bf16),
            pltpu.VMEM((w_out.shape[0] // 2, w_out.shape[1]), bf16),
        ],
        scratch_shapes=[pltpu.SemaphoreType.DMA((8,))],
        compiler_params=params(16),
        cost_estimate=FAR_APART,
        name="attention",
    )(level_weights, prior_states, in_hbm(w_out), after, qt_old, raw, keys, values_t)


def far_body(width, first_level, halves, counts, first, number, after, *refs):
    refs = list(refs)
    qt_refs = [refs.pop(0) for _ in range(halves)]
    acc_ref = refs.pop(0)
    arrived = [[refs.pop(0) for _ in range(count)] for count in counts]
    lam_ref, gain_ref, out_ref = refs
    nbits = len(counts) // 2
    heads = lam_ref.shape[1]
    half = heads // 2
    per = heads // halves
    mine = lax.axis_index("seq")
    odd = (mine & 1) > 0

    def state(pieces, n):
        each = pieces[0].shape[0]
        return pieces[n // each][n % each]

    for head in range(heads):
        own = slice(head * width, (head + 1) * width)
        states = []
        for j in range(nbits):
            kept, swapped = state(arrived[2 * j], head % half), state(arrived[2 * j + 1], head % half)
            if j == 0:
                states.append(kept if head >= half else swapped)
            else:
                states.append(jnp.where(odd, kept, swapped) if head >= half else jnp.where(odd, swapped, kept))
        states = jnp.concatenate(states, axis=0)
        for i in range(number):
            tile = first + i
            qt = qt_refs[head // per][tile, head % per * width : (head % per + 1) * width, :]
            product = mm(states, qt)
            total = acc_ref[tile, own, :]
            for j in range(nbits):
                lam = lam_ref[first_level + j, head : head + 1, tile * TILE : (tile + 1) * TILE]
                lam = jnp.where(((mine >> j) & 1) > 0, lam, 0.0)
                total = total + lam * product[j * width : (j + 1) * width]
            scale = lax.rsqrt(jnp.mean(total * total, axis=0, keepdims=True) + eps)
            out_ref[i * TILE : (i + 1) * TILE, own] = ((total * scale).T * gain_ref[:, own]).astype(bf16)


def far_part(after, queries_t, acc, states, level_weights, gain, width, first, number):
    levels, heads, rows = level_weights.shape
    total = heads * width
    halves = len(queries_t)
    counts = [len(pieces) for pieces in states]
    states = [piece for pieces in states for piece in pieces]
    return pl.pallas_call(
        functools.partial(far_body, width, rows.bit_length(), halves, counts, first, number),
        in_specs=[ANY] + [VMEM] * (halves + 3 + len(states)),
        out_specs=VMEM,
        out_shape=pltpu.VMEM((number * TILE, total), bf16),
        compiler_params=params(16),
        cost_estimate=cost(8 * rows * width * total, 8 * rows * total),
        name="far_part",
    )(after, *queries_t, acc, *states, level_weights, gain)


def project_body(flip, d, groups, start, take, count, after, w_top, w_low, *refs):
    pieces, added, out_ref = refs[:count], refs[count:-1], refs[-1]
    columns = out_ref.shape[1]
    depth = w_top.shape[0]
    base = lax.rem((lax.axis_index("head") ^ flip) + 2 * d, groups) * columns
    step = min(512, columns)
    for first in range(0, columns, step):
        here = slice(first, first + step)
        there = pl.ds(pl.multiple_of(base + first, 128), step)
        top, low = w_top[:, there], w_low[:, there]
        row = 0
        for a in pieces:
            some = take or a.shape[0]
            total = mm(a[start : start + some, :depth], top) + mm(a[start : start + some, depth:], low)
            for ref in added:
                total = total + ref[start : start + some, here].astype(f32)
            out_ref[row : row + some, here] = total.astype(out_ref.dtype)
            row += some


def project(after, weights, flip, d, groups, pieces, kind, start=0, take=None, added=(), estimate=None):
    depth, columns = weights[0].shape
    columns //= groups
    total = take or sum(a.shape[0] for a in pieces)
    return pl.pallas_call(
        functools.partial(project_body, flip, d, groups, start, take, len(pieces)),
        in_specs=[ANY, VMEM, VMEM] + [VMEM] * (len(pieces) + len(added)),
        out_specs=VMEM,
        out_shape=pltpu.VMEM((total, columns), kind),
        compiler_params=params(16),
        cost_estimate=estimate or cost(4 * total * depth * columns, 4 * depth * columns),
        name="project",
    )(after, *weights, *pieces, *added)


def finish_body(out_in, own_ref, *refs):
    out_ref = refs[-1]
    total = own_ref[...]
    for ref in refs[:-1]:
        total = total + ref[...].astype(f32)
    out_ref[...] = total.astype(bf16)


def finish(out, own, other, terms, first):
    rows, columns = own.shape
    place = lambda i: (first // TILE + i, 0)
    return pl.pallas_call(
        finish_body,
        grid=(terms[0].shape[0] // TILE,),
        in_specs=[ANY] + [pl.BlockSpec((TILE, columns), place)] * 2
        + [pl.BlockSpec((TILE, columns), lambda i: (i, 0))] * len(terms),
        out_specs=pl.BlockSpec((TILE, columns), place),
        out_shape=jax.ShapeDtypeStruct((rows, columns), bf16),
        input_output_aliases={0: 0} if first else {},
        compiler_params=params(16),
        cost_estimate=FAR_APART,
        name="finish",
    )(out, own, other, *terms)


def per_device(tokens, w_query, w_key, w_value, w_out, norm_gain, level_weights, prior_states):
    levels, heads, rows = level_weights.shape
    width = prior_states.shape[-1]
    count = lax.axis_size("seq")
    nbits = count.bit_length() - 1
    groups = lax.axis_size("head")
    chips = groups // 2
    twin = [(i, i ^ 1) for i in range(groups)]
    gain = norm_gain.reshape(1, heads * width)

    def send(state, j):
        return lax.ppermute(state, "seq", [(r, r ^ (1 << j)) for r in range(count)])

    def merge(state, got):
        return (state.astype(f32) + got.astype(f32)).astype(bf16)

    def not_before(value, done):
        return lax.optimization_barrier((value, done))[0]

    tokens, half_query, keys, values_t, keep, give = keys_values(tokens, w_key, w_value, w_query, width)
    got = send(give, 0)
    raw_a, next_query, level_weights, prior_states = queries_first(
        tokens, half_query, w_query, level_weights, prior_states, keep
    )
    got = not_before(got, raw_a)
    running = merge(keep, got)
    kept, swapped = [[got]], []
    for j in range(1, nbits):
        cut = running.shape[0]
        gots = [send(running[n : n + cut], j) for n in range(0, running.shape[0], cut)]
        if j == 1:
            q_a, done, w_top = queries_second(tokens, next_query, raw_a, w_out, running, width)
        if j == nbits - 1:
            acc, q_b, w_low = attention(
                q_a, done, keys, values_t, level_weights, prior_states, w_out, running, width
            )
            swapped = [[send(not_before(keep, running), 0)]] + [[send(not_before(old[0], running), 0)] for old in kept[1:]]
            done = acc
        gots = [not_before(got, done) for got in gots]
        if j < nbits - 1:
            running = merge(running, gots[0])
        kept.append(gots)
    swapped.append([send(got, 0) for got in kept[-1]])
    states = [pieces for pair in zip(kept, swapped) for pieces in pair]
    queries_t = [q_a, q_b]
    weights = (w_top, w_low)

    def shared(after, piece):
        gots = []
        for d in range(1, chips):
            after = project(after, weights, 1, d, groups, [piece], bf16)
            gots.append(lax.ppermute(after, "head", twin))
        return after, gots

    received = []

    def onward(after, piece, gots, start, take, estimate=None):
        terms = []
        for d in range(1, chips):
            after = project(after, weights, 0, d, groups, [piece], bf16, start, take, gots[d - 1 : d], estimate)
            terms.append(lax.ppermute(after, "head", [(i, (i + 2 * d) % groups) for i in range(groups)]))
        received.append(terms)
        return after

    ahead = far_part(acc, queries_t, acc, states, level_weights, gain, width, 0, 1)
    after, ahead_gots = shared(ahead, ahead)
    rest = far_part(after, queries_t, acc, states, level_weights, gain, width, 1, rows // TILE - 1)
    after = onward(rest, ahead, ahead_gots, 0, TILE)
    after, rest_gots = shared(after, rest)
    after = project(after, weights, 1, 0, groups, [ahead, rest], bf16, estimate=FAR_APART)
    other = lax.ppermute(after, "head", twin)
    after = onward(after, rest, rest_gots, 0, rows - 2 * TILE, FAR_APART)
    after = onward(after, rest, rest_gots, rows - 2 * TILE, TILE)
    own = project(after, weights, 0, 0, groups, [ahead, rest], f32)
    out = finish(gain, own, other, received[0], 0)
    out = finish(out, own, other, received[1], TILE)
    return finish(out, own, other, received[2], rows - TILE)


def solution(mesh):
    placed = (
        P("seq", None),
        P(None, "head"),
        P(None, "head"),
        P(None, "head"),
        P("head", None),
        P("head"),
        P(None, "head", "seq"),
        P(None, "head", None, None),
    )
    return jax.shard_map(
        per_device, mesh=mesh, in_specs=placed, out_specs=P("seq", "head"), check_vma=False
    )
```

```python
import functools

import jax
import jax.numpy as jnp
from jax import lax
from jax.experimental import pallas as pl
from jax.experimental.pallas import tpu as pltpu
from jax.sharding import PartitionSpec as P

eps = 1e-06
TILE = 128
MIB = 1024 * 1024
f32, bf16 = jnp.float32, jnp.bfloat16
HBM = pl.BlockSpec(memory_space=pltpu.HBM)
VMEM = pl.BlockSpec(memory_space=pltpu.VMEM)
SMEM = pl.BlockSpec(memory_space=pltpu.SMEM)
ANY = pl.BlockSpec(memory_space=pl.ANY)


def mm(a, b):
    return jnp.dot(a, b, preferred_element_type=f32)


def params(mib):
    return pltpu.CompilerParams(vmem_limit_bytes=mib * MIB)


def cost(flops, size):
    return pl.CostEstimate(flops=int(flops) // 100, bytes_accessed=int(size) // 100, transcendentals=0)


FAR_APART = pl.CostEstimate(flops=4 * 10**10, bytes_accessed=10**8, transcendentals=0)


def in_hbm(x):
    return pltpu.with_memory_space_constraint(x, pltpu.HBM)


def starts(copies):
    for copy in copies:
        copy.start()


def keys_values_body(
    width, x_hbm, wk_hbm, wv_hbm, wq_hbm, x, wq, k_ref, vt_ref, keep_ref, give_ref, wk, wv, k_acc, v_acc, s, sem
):
    rows, depth = x.shape
    size = wk.shape[1]
    cuts = sem.shape[1]
    cut = depth // cuts
    at = [pl.ds(c * cut, cut) for c in range(cuts)]
    x_in = [pltpu.make_async_copy(x_hbm.at[:, a], x.at[:, a], sem.at[0, c]) for c, a in enumerate(at)]
    v_in = [pltpu.make_async_copy(wv_hbm.at[a], wv.at[a], sem.at[1, c]) for c, a in enumerate(at)]
    k_in = [pltpu.make_async_copy(wk_hbm.at[a], wk.at[a], sem.at[2, c]) for c, a in enumerate(at)]
    q_in = [pltpu.make_async_copy(wq_hbm.at[a], wq.at[a], sem.at[3, c]) for c, a in enumerate(at)]
    for c in range(cuts):
        starts((x_in[c], v_in[c]))
    starts(k_in)
    starts(q_in)
    heads = size // width
    half = heads // 2
    own = [slice(h * width, (h + 1) * width) for h in range(heads)]
    for c, a in enumerate(at):
        x_in[c].wait()
        v_in[c].wait()
        term = mm(x[:, a], wv[a, :])
        v_acc[...] = term if c == 0 else v_acc[...] + term
    for c, a in enumerate(at):
        k_in[c].wait()
        term = mm(x[:, a], wk[a, :])
        k_acc[...] = term if c == 0 else k_acc[...] + term
        for h in range(c * heads // cuts, (c + 1) * heads // cuts):
            vt_ref[own[h], :] = v_acc[:, own[h]].T.astype(bf16)
    for h in range(heads):
        raw = k_acc[:, own[h]]
        key = (raw * lax.rsqrt(jnp.sum(raw * raw, axis=-1, keepdims=True) + eps)).astype(bf16)
        k_ref[:, own[h]] = key
        s[h] = mm(vt_ref[own[h], :], key).astype(bf16)
    first = (lax.axis_index("seq") & 1) * half
    for h in range(half):
        keep_ref[h] = s[first + h]
        give_ref[h] = s[half - first + h]
    for copy in q_in:
        copy.wait()


def keys_values(tokens, w_key, w_value, w_query, width):
    rows, depth = tokens.shape
    size = w_key.shape[1]
    heads = size // width
    cuts = 8
    part = pltpu.VMEM((heads // 2, width, width), bf16)
    return pl.pallas_call(
        functools.partial(keys_values_body, width),
        in_specs=[HBM] * 4,
        out_specs=[VMEM] * 6,
        out_shape=[
            pltpu.VMEM((rows, depth), bf16),
            pltpu.VMEM((depth, size), bf16),
            pltpu.VMEM((rows, size), bf16),
            pltpu.VMEM((size, rows), bf16),
            part,
            part,
        ],
        scratch_shapes=[
            pltpu.VMEM((depth, size), bf16),
            pltpu.VMEM((depth, size), bf16),
            pltpu.VMEM((rows, size), f32),
            pltpu.VMEM((rows, size), f32),
            pltpu.VMEM((heads, width, width), bf16),
            pltpu.SemaphoreType.DMA((4, cuts)),
        ],
        compiler_params=params(30),
        cost_estimate=cost(4 * rows * depth * size, 2 * (rows * depth + 2 * depth * size)),
        name="keys_values",
    )(in_hbm(tokens), in_hbm(w_key), in_hbm(w_value), in_hbm(w_query))


def attend(qt, k, vt, lam, prior):
    width, rows = qt.shape
    shift = rows.bit_length() - 1
    low = TILE.bit_length() - 1
    levels, priors = lam.shape[0], len(prior)
    product = mm(jnp.concatenate([p.astype(bf16).T for p in prior], axis=0), qt)
    total = lam[levels - priors : levels - priors + 1] * product[:width]
    for p in range(1, priors):
        lv = levels - priors + p
        total = total + lam[lv : lv + 1] * product[p * width : (p + 1) * width]
    t_at = lax.broadcasted_iota(jnp.int32, (8, rows), 1) & 7
    s_at = lax.broadcasted_iota(jnp.int32, (8, rows), 0)
    near = jnp.zeros((8, rows), f32)
    for lv in range(4):
        picked = (t_at ^ s_at) >= (1 << lv >> 1)
        near = jnp.where(picked, lam[lv : lv + 1], near)
    near = jnp.where(s_at <= t_at, near, 0.0)
    groups = TILE // 8
    t_group = (lax.broadcasted_iota(jnp.int32, (groups, rows), 1) & (TILE - 1)) >> 3
    s_group = lax.broadcasted_iota(jnp.int32, (groups, rows), 0)
    wide = jnp.zeros((groups, rows), f32)
    for lv in range(4, low + 1):
        picked = (t_group ^ s_group) >= (1 << (lv - 4))
        wide = jnp.where(picked, lam[lv : lv + 1], wide)
    wide = jnp.where(s_group < t_group, wide, 0.0)
    lane_group = (lax.broadcasted_iota(jnp.int32, (8, TILE), 1)) >> 3
    pieces = []
    for i in range(rows // TILE):
        here = slice(i * TILE, (i + 1) * TILE)
        scores = mm(k[here], qt[:, here])
        mixing = []
        for g in range(groups):
            weight = jnp.where(lane_group == g, near[:, here], wide[g : g + 1, here])
            mixing.append(weight * scores[g * 8 : g * 8 + 8])
        mixing = jnp.concatenate(mixing, axis=0).astype(bf16)
        pieces.append(total[:, here] + mm(vt[:, here], mixing))
    for bit in range(low, shift):
        half = 1 << bit
        for start in range(half, rows, 2 * half):
            past = slice(start - half, start)
            here = slice(start, start + half)
            state = mm(vt[:, past], k[past]).astype(bf16)
            found = lam[1 + bit : 2 + bit, here] * mm(state, qt[:, here])
            for n in range(half // TILE):
                i = start // TILE + n
                pieces[i] = pieces[i] + found[:, n * TILE : (n + 1) * TILE]
    return pieces


def whole(qt_ref, at):
    return jnp.concatenate([qt_ref[i, at, :] for i in range(qt_ref.shape[0])], axis=1)


def finished(raw):
    raw = raw.T
    return (raw * lax.rsqrt(jnp.sum(raw * raw, axis=0, keepdims=True) + eps)).astype(bf16)


def leave_tiles(ref, at, qt):
    for i in range(ref.shape[0]):
        ref[i, at, :] = qt[:, i * TILE : (i + 1) * TILE]


def row_copies(source, first, target, sem, at, pieces):
    cut = target.shape[0] // pieces
    return [
        pltpu.make_async_copy(source.at[pl.ds(first + c * cut, cut)], target.at[pl.ds(c * cut, cut)], sem.at[at + c])
        for c in range(pieces)
    ]


def query_product(x, wq, raw_ref, first, meanwhile):
    rows, depth = x.shape
    size = raw_ref.shape[1]
    cuts = 8
    cut = depth // cuts
    for c in range(cuts):
        a = slice(c * cut, (c + 1) * cut)
        term = mm(x[:, a], wq[a, first : first + size])
        raw_ref[...] = term if c == 0 else raw_ref[...] + term
        meanwhile(c, cuts)


def queries_first_body(x, wq, lam_hbm, prior_hbm, after, raw_ref, lam, prior, sem):
    copies = [pltpu.make_async_copy(lam_hbm, lam, sem.at[0])]
    heads = prior.shape[1]
    for p in range(prior.shape[0]):
        for h in range(heads):
            copies.append(pltpu.make_async_copy(prior_hbm.at[p, h], prior.at[p, h], sem.at[1 + p * heads + h]))
    starts(copies)
    query_product(x, wq, raw_ref, 0, lambda c, cuts: None)
    for copy in copies:
        copy.wait()


def queries_first(tokens, w_query, level_weights, prior_states, after):
    rows, depth = tokens.shape
    size = w_query.shape[1] // 2
    priors, heads = prior_states.shape[:2]
    return pl.pallas_call(
        queries_first_body,
        in_specs=[VMEM, VMEM, HBM, HBM, ANY],
        out_specs=[VMEM] * 3,
        out_shape=[
            pltpu.VMEM((rows, size), f32),
            pltpu.VMEM(level_weights.shape, f32),
            pltpu.VMEM(prior_states.shape, f32),
        ],
        scratch_shapes=[pltpu.SemaphoreType.DMA((1 + priors * heads,))],
        compiler_params=params(16),
        cost_estimate=cost(2 * rows * depth * size, 2 * (rows * depth + depth * size)),
        name="queries_first",
    )(tokens, w_query, in_hbm(level_weights), in_hbm(prior_states), after)


def queries_second_body(width, x, wq, raw_old, w_hbm, after, qt_ref, raw_ref, w_ref, sem):
    copies = row_copies(w_hbm, 0, w_ref, sem, 0, sem.shape[0])
    starts(copies)
    heads = raw_old.shape[1] // width

    def meanwhile(c, cuts):
        for h in range(c * heads // cuts, (c + 1) * heads // cuts):
            own = slice(h * width, (h + 1) * width)
            leave_tiles(qt_ref, own, finished(raw_old[:, own]))

    query_product(x, wq, raw_ref, raw_old.shape[1], meanwhile)
    for copy in copies:
        copy.wait()


def queries_second(tokens, w_query, raw_old, w_out, after, width):
    rows, depth = tokens.shape
    size = w_query.shape[1] // 2
    return pl.pallas_call(
        functools.partial(queries_second_body, width),
        in_specs=[VMEM, VMEM, VMEM, HBM, ANY],
        out_specs=[VMEM] * 3,
        out_shape=[
            pltpu.VMEM((rows // TILE, size, TILE), bf16),
            pltpu.VMEM((rows, size), f32),
            pltpu.VMEM((w_out.shape[0] // 2, w_out.shape[1]), bf16),
        ],
        scratch_shapes=[pltpu.SemaphoreType.DMA((w_out.shape[0] // 32,))],
        compiler_params=params(16),
        cost_estimate=cost(2 * rows * depth * size, 2 * (rows * depth + depth * size)),
        name="queries_second",
    )(tokens, w_query, raw_old, in_hbm(w_out), after)


def attention_body(width, lam_ref, prior_ref, after, qt_old, raw, k_ref, vt_ref, acc_ref, qt_ref):
    heads = prior_ref.shape[1]
    per = heads // 2
    for h in range(heads):
        own = slice(h % per * width, (h % per + 1) * width)
        every = slice(h * width, (h + 1) * width)
        if h < per:
            qt = whole(qt_old, own)
        else:
            qt = finished(raw[:, own])
            leave_tiles(qt_ref, own, qt)
        prior = [prior_ref[p, h] for p in range(prior_ref.shape[0])]
        pieces = attend(qt, k_ref[:, every], vt_ref[every, :], lam_ref[:, h, :], prior)
        for i, piece in enumerate(pieces):
            acc_ref[i, every, :] = piece


def attention(qt_old, raw, keys, values_t, level_weights, prior_states, after, width):
    tiles, size, take = qt_old.shape
    return pl.pallas_call(
        functools.partial(attention_body, width),
        in_specs=[VMEM] * 2 + [ANY] + [VMEM] * 4,
        out_specs=[VMEM] * 2,
        out_shape=[pltpu.VMEM((tiles, 2 * size, take), f32), pltpu.VMEM(qt_old.shape, bf16)],
        compiler_params=params(16),
        cost_estimate=FAR_APART,
        name="attention",
    )(level_weights, prior_states, after, qt_old, raw, keys, values_t)


def fetch_body(w_hbm, *refs):
    w_ref, sem = refs[-2:]
    copies = row_copies(w_hbm, w_ref.shape[0], w_ref, sem, 0, sem.shape[0])
    starts(copies)
    for copy in copies:
        copy.wait()


def fetch(w_out, after):
    depth, total = w_out.shape
    return pl.pallas_call(
        fetch_body,
        in_specs=[HBM] + [ANY] * len(after),
        out_specs=VMEM,
        out_shape=pltpu.VMEM((depth // 2, total), bf16),
        scratch_shapes=[pltpu.SemaphoreType.DMA((depth // 32,))],
        compiler_params=params(4),
        cost_estimate=cost(0, 2 * depth * total),
        name="fetch",
    )(in_hbm(w_out), *after)


def far_body(width, first_level, halves, counts, first, number, after, *refs):
    refs = list(refs)
    qt_refs = [refs.pop(0) for _ in range(halves)]
    acc_ref = refs.pop(0)
    arrived = [[refs.pop(0) for _ in range(count)] for count in counts]
    lam_ref, gain_ref, out_ref = refs
    nbits = len(counts) // 2
    heads = lam_ref.shape[1]
    half = heads // 2
    per = heads // halves
    mine = lax.axis_index("seq")
    odd = (mine & 1) > 0

    def state(pieces, n):
        each = pieces[0].shape[0]
        return pieces[n // each][n % each]

    for head in range(heads):
        own = slice(head * width, (head + 1) * width)
        states = []
        for j in range(nbits):
            kept, swapped = state(arrived[2 * j], head % half), state(arrived[2 * j + 1], head % half)
            if j == 0:
                states.append(kept if head >= half else swapped)
            else:
                states.append(jnp.where(odd, kept, swapped) if head >= half else jnp.where(odd, swapped, kept))
        states = jnp.concatenate(states, axis=0)
        for i in range(number):
            tile = first + i
            qt = qt_refs[head // per][tile, head % per * width : (head % per + 1) * width, :]
            product = mm(states, qt)
            total = acc_ref[tile, own, :]
            for j in range(nbits):
                lam = lam_ref[first_level + j, head : head + 1, tile * TILE : (tile + 1) * TILE]
                lam = jnp.where(((mine >> j) & 1) > 0, lam, 0.0)
                total = total + lam * product[j * width : (j + 1) * width]
            scale = lax.rsqrt(jnp.mean(total * total, axis=0, keepdims=True) + eps)
            out_ref[i * TILE : (i + 1) * TILE, own] = ((total * scale).T * gain_ref[:, own]).astype(bf16)


def far_part(after, queries_t, acc, states, level_weights, gain, width, first, number):
    levels, heads, rows = level_weights.shape
    total = heads * width
    halves = len(queries_t)
    counts = [len(pieces) for pieces in states]
    states = [piece for pieces in states for piece in pieces]
    return pl.pallas_call(
        functools.partial(far_body, width, rows.bit_length(), halves, counts, first, number),
        in_specs=[ANY] + [VMEM] * (halves + 3 + len(states)),
        out_specs=VMEM,
        out_shape=pltpu.VMEM((number * TILE, total), bf16),
        compiler_params=params(16),
        cost_estimate=cost(8 * rows * width * total, 8 * rows * total),
        name="far_part",
    )(after, *queries_t, acc, *states, level_weights, gain)


def project_body(flip, d, groups, start, take, count, after, w_top, w_low, *refs):
    pieces, added, out_ref = refs[:count], refs[count:-1], refs[-1]
    columns = out_ref.shape[1]
    depth = w_top.shape[0]
    base = lax.rem((lax.axis_index("head") ^ flip) + 2 * d, groups) * columns
    step = min(512, columns)
    for first in range(0, columns, step):
        here = slice(first, first + step)
        there = pl.ds(pl.multiple_of(base + first, 128), step)
        top, low = w_top[:, there], w_low[:, there]
        row = 0
        for a in pieces:
            some = take or a.shape[0]
            total = mm(a[start : start + some, :depth], top) + mm(a[start : start + some, depth:], low)
            for ref in added:
                total = total + ref[start : start + some, here].astype(f32)
            out_ref[row : row + some, here] = total.astype(out_ref.dtype)
            row += some


def project(after, weights, flip, d, groups, pieces, kind, start=0, take=None, added=(), estimate=None):
    depth, columns = weights[0].shape
    columns //= groups
    total = take or sum(a.shape[0] for a in pieces)
    return pl.pallas_call(
        functools.partial(project_body, flip, d, groups, start, take, len(pieces)),
        in_specs=[ANY, VMEM, VMEM] + [VMEM] * (len(pieces) + len(added)),
        out_specs=VMEM,
        out_shape=pltpu.VMEM((total, columns), kind),
        compiler_params=params(16),
        cost_estimate=estimate or cost(4 * total * depth * columns, 4 * depth * columns),
        name="project",
    )(after, *weights, *pieces, *added)


def finish_body(out_in, own_ref, *refs):
    out_ref = refs[-1]
    total = own_ref[...]
    for ref in refs[:-1]:
        total = total + ref[...].astype(f32)
    out_ref[...] = total.astype(bf16)


def finish(out, own, other, terms, first):
    rows, columns = own.shape
    place = lambda i: (first // TILE + i, 0)
    return pl.pallas_call(
        finish_body,
        grid=(terms[0].shape[0] // TILE,),
        in_specs=[ANY] + [pl.BlockSpec((TILE, columns), place)] * 2
        + [pl.BlockSpec((TILE, columns), lambda i: (i, 0))] * len(terms),
        out_specs=pl.BlockSpec((TILE, columns), place),
        out_shape=jax.ShapeDtypeStruct((rows, columns), bf16),
        input_output_aliases={0: 0} if first else {},
        compiler_params=params(16),
        cost_estimate=FAR_APART,
        name="finish",
    )(out, own, other, *terms)


def per_device(tokens, w_query, w_key, w_value, w_out, norm_gain, level_weights, prior_states):
    levels, heads, rows = level_weights.shape
    width = prior_states.shape[-1]
    count = lax.axis_size("seq")
    nbits = count.bit_length() - 1
    groups = lax.axis_size("head")
    chips = groups // 2
    twin = [(i, i ^ 1) for i in range(groups)]
    gain = norm_gain.reshape(1, heads * width)

    def send(state, j):
        return lax.ppermute(state, "seq", [(r, r ^ (1 << j)) for r in range(count)])

    def merge(state, got):
        return (state.astype(f32) + got.astype(f32)).astype(bf16)

    def not_before(value, done):
        return lax.optimization_barrier((value, done))[0]

    tokens, w_query, keys, values_t, keep, give = keys_values(tokens, w_key, w_value, w_query, width)
    got = send(give, 0)
    raw_a, level_weights, prior_states = queries_first(tokens, w_query, level_weights, prior_states, keep)
    got = not_before(got, raw_a)
    running = merge(keep, got)
    kept, swapped = [[got]], []
    for j in range(1, nbits):
        gots = [send(running, j)]
        if j == 1:
            q_a, done, w_top = queries_second(tokens, w_query, raw_a, w_out, running, width)
        if j == nbits - 1:
            acc, q_b = attention(q_a, done, keys, values_t, level_weights, prior_states, running, width)
            swapped = [[send(not_before(keep, running), 0)]] + [[send(not_before(old[0], running), 0)] for old in kept[1:]]
            done = acc
        gots = [not_before(got, done) for got in gots]
        if j < nbits - 1:
            running = merge(running, gots[0])
        kept.append(gots)
    w_low = fetch(w_out, [pieces[0] for pieces in kept[-1:] + swapped])
    swapped.append([not_before(send(got, 0), w_low) for got in kept[-1]])
    states = [pieces for pair in zip(kept, swapped) for pieces in pair]
    queries_t = [q_a, q_b]
    weights = (w_top, w_low)

    def shared(after, piece):
        gots = []
        for d in range(1, chips):
            after = project(after, weights, 1, d, groups, [piece], bf16)
            gots.append(lax.ppermute(after, "head", twin))
        return after, gots

    received = []

    def onward(after, piece, gots, start, take, estimate=None):
        terms = []
        for d in range(1, chips):
            after = project(after, weights, 0, d, groups, [piece], bf16, start, take, gots[d - 1 : d], estimate)
            terms.append(lax.ppermute(after, "head", [(i, (i + 2 * d) % groups) for i in range(groups)]))
        received.append(terms)
        return after

    ahead = far_part(acc, queries_t, acc, states, level_weights, gain, width, 0, 1)
    after, ahead_gots = shared(ahead, ahead)
    rest = far_part(after, queries_t, acc, states, level_weights, gain, width, 1, rows // TILE - 1)
    after = onward(rest, ahead, ahead_gots, 0, TILE)
    after, rest_gots = shared(after, rest)
    after = project(after, weights, 1, 0, groups, [ahead, rest], bf16, estimate=FAR_APART)
    other = lax.ppermute(after, "head", twin)
    after = onward(after, rest, rest_gots, 0, rows - 2 * TILE, FAR_APART)
    after = onward(after, rest, rest_gots, rows - 2 * TILE, TILE)
    own = project(after, weights, 0, 0, groups, [ahead, rest], f32)
    out = finish(gain, own, other, received[0], 0)
    out = finish(out, own, other, received[1], TILE)
    return finish(out, own, other, received[2], rows - TILE)


def solution(mesh):
    placed = (
        P("seq", None),
        P(None, "head"),
        P(None, "head"),
        P(None, "head"),
        P("head", None),
        P("head"),
        P(None, "head", "seq"),
        P(None, "head", None, None),
    )
    return jax.shard_map(
        per_device, mesh=mesh, in_specs=placed, out_specs=P("seq", "head"), check_vma=False
    )
```

```python
import functools

import jax
import jax.numpy as jnp
from jax import lax
from jax.experimental import pallas as pl
from jax.experimental.pallas import tpu as pltpu
from jax.sharding import PartitionSpec as P

eps = 1e-06
TILE = 128
MIB = 1024 * 1024
f32, bf16 = jnp.float32, jnp.bfloat16
HBM = pl.BlockSpec(memory_space=pltpu.HBM)
VMEM = pl.BlockSpec(memory_space=pltpu.VMEM)
SMEM = pl.BlockSpec(memory_space=pltpu.SMEM)
ANY = pl.BlockSpec(memory_space=pl.ANY)


def mm(a, b):
    return jnp.dot(a, b, preferred_element_type=f32)


def params(mib):
    return pltpu.CompilerParams(vmem_limit_bytes=mib * MIB)


def cost(flops, size):
    return pl.CostEstimate(flops=int(flops) // 100, bytes_accessed=int(size) // 100, transcendentals=0)


FAR_APART = pl.CostEstimate(flops=4 * 10**10, bytes_accessed=10**8, transcendentals=0)


def in_hbm(x):
    return pltpu.with_memory_space_constraint(x, pltpu.HBM)


def starts(copies):
    for copy in copies:
        copy.start()


def keys_values_body(
    width, x_hbm, wk_hbm, wv_hbm, wq_hbm, x, wq, k_ref, vt_ref, keep_ref, give_ref, wk, wv, k_acc, v_acc, s, vt, sem, vt_sem
):
    rows, depth = x.shape
    size = wk.shape[1]
    cuts = sem.shape[1]
    cut = depth // cuts
    at = [pl.ds(c * cut, cut) for c in range(cuts)]
    x_in = [pltpu.make_async_copy(x_hbm.at[:, a], x.at[:, a], sem.at[0, c]) for c, a in enumerate(at)]
    v_in = [pltpu.make_async_copy(wv_hbm.at[a], wv.at[a], sem.at[1, c]) for c, a in enumerate(at)]
    k_in = [pltpu.make_async_copy(wk_hbm.at[a], wk.at[a], sem.at[2, c]) for c, a in enumerate(at)]
    q_in = [pltpu.make_async_copy(wq_hbm.at[a], wq.at[a], sem.at[3, c]) for c, a in enumerate(at)]
    for c in range(cuts):
        starts((x_in[c], v_in[c]))
    starts(k_in)
    starts(q_in)
    heads = size // width
    half = heads // 2
    own = [slice(h * width, (h + 1) * width) for h in range(heads)]
    for c, a in enumerate(at):
        x_in[c].wait()
        v_in[c].wait()
        term = mm(x[:, a], wv[a, :])
        v_acc[...] = term if c == 0 else v_acc[...] + term
    for c, a in enumerate(at):
        k_in[c].wait()
        term = mm(x[:, a], wk[a, :])
        k_acc[...] = term if c == 0 else k_acc[...] + term
        for h in range(c * heads // cuts, (c + 1) * heads // cuts):
            vt[own[h], :] = v_acc[:, own[h]].T.astype(bf16)
    vt_out = pltpu.make_async_copy(vt, vt_ref, vt_sem)
    vt_out.start()
    for h in range(heads):
        raw = k_acc[:, own[h]]
        key = (raw * lax.rsqrt(jnp.sum(raw * raw, axis=-1, keepdims=True) + eps)).astype(bf16)
        k_ref[:, own[h]] = key
        s[h] = mm(vt[own[h], :], key).astype(bf16)
    first = (lax.axis_index("seq") & 1) * half
    for h in range(half):
        keep_ref[h] = s[first + h]
        give_ref[h] = s[half - first + h]
    for copy in q_in:
        copy.wait()
    vt_out.wait()


def keys_values(tokens, w_key, w_value, w_query, width):
    rows, depth = tokens.shape
    size = w_key.shape[1]
    heads = size // width
    cuts = 8
    part = pltpu.VMEM((heads // 2, width, width), bf16)
    return pl.pallas_call(
        functools.partial(keys_values_body, width),
        in_specs=[HBM] * 4,
        out_specs=[VMEM] * 6,
        out_shape=[
            pltpu.VMEM((rows, depth), bf16),
            pltpu.VMEM((depth, size), bf16),
            pltpu.VMEM((rows, size), bf16),
            pltpu.VMEM((size, rows), bf16),
            part,
            part,
        ],
        scratch_shapes=[
            pltpu.VMEM((depth, size), bf16),
            pltpu.VMEM((depth, size), bf16),
            pltpu.VMEM((rows, size), f32),
            pltpu.VMEM((rows, size), f32),
            pltpu.VMEM((heads, width, width), bf16),
            pltpu.VMEM((size, rows), bf16),
            pltpu.SemaphoreType.DMA((4, cuts)),
            pltpu.SemaphoreType.DMA,
        ],
        compiler_params=params(34),
        cost_estimate=cost(4 * rows * depth * size, 2 * (rows * depth + 2 * depth * size)),
        name="keys_values",
    )(in_hbm(tokens), in_hbm(w_key), in_hbm(w_value), in_hbm(w_query))


def attend(qt, k, vt, lam, prior):
    width, rows = qt.shape
    shift = rows.bit_length() - 1
    low = TILE.bit_length() - 1
    levels, priors = lam.shape[0], len(prior)
    product = mm(jnp.concatenate([p.astype(bf16).T for p in prior], axis=0), qt)
    total = lam[levels - priors : levels - priors + 1] * product[:width]
    for p in range(1, priors):
        lv = levels - priors + p
        total = total + lam[lv : lv + 1] * product[p * width : (p + 1) * width]
    t_at = lax.broadcasted_iota(jnp.int32, (8, rows), 1) & 7
    s_at = lax.broadcasted_iota(jnp.int32, (8, rows), 0)
    near = jnp.zeros((8, rows), f32)
    for lv in range(4):
        picked = (t_at ^ s_at) >= (1 << lv >> 1)
        near = jnp.where(picked, lam[lv : lv + 1], near)
    near = jnp.where(s_at <= t_at, near, 0.0)
    groups = TILE // 8
    t_group = (lax.broadcasted_iota(jnp.int32, (groups, rows), 1) & (TILE - 1)) >> 3
    s_group = lax.broadcasted_iota(jnp.int32, (groups, rows), 0)
    wide = jnp.zeros((groups, rows), f32)
    for lv in range(4, low + 1):
        picked = (t_group ^ s_group) >= (1 << (lv - 4))
        wide = jnp.where(picked, lam[lv : lv + 1], wide)
    wide = jnp.where(s_group < t_group, wide, 0.0)
    lane_group = (lax.broadcasted_iota(jnp.int32, (8, TILE), 1)) >> 3
    pieces = []
    for i in range(rows // TILE):
        here = slice(i * TILE, (i + 1) * TILE)
        scores = mm(k[here], qt[:, here])
        mixing = []
        for g in range(groups):
            weight = jnp.where(lane_group == g, near[:, here], wide[g : g + 1, here])
            mixing.append(weight * scores[g * 8 : g * 8 + 8])
        mixing = jnp.concatenate(mixing, axis=0).astype(bf16)
        pieces.append(total[:, here] + mm(vt[:, here], mixing))
    for bit in range(low, shift):
        half = 1 << bit
        for start in range(half, rows, 2 * half):
            past = slice(start - half, start)
            here = slice(start, start + half)
            state = mm(vt[:, past], k[past]).astype(bf16)
            found = lam[1 + bit : 2 + bit, here] * mm(state, qt[:, here])
            for n in range(half // TILE):
                i = start // TILE + n
                pieces[i] = pieces[i] + found[:, n * TILE : (n + 1) * TILE]
    return pieces


def whole(qt_ref, at):
    return jnp.concatenate([qt_ref[i, at, :] for i in range(qt_ref.shape[0])], axis=1)


def finished(raw):
    raw = raw.T
    return (raw * lax.rsqrt(jnp.sum(raw * raw, axis=0, keepdims=True) + eps)).astype(bf16)


def leave_tiles(ref, at, qt):
    for i in range(ref.shape[0]):
        ref[i, at, :] = qt[:, i * TILE : (i + 1) * TILE]


def row_copies(source, first, target, sem, at, pieces):
    cut = target.shape[0] // pieces
    return [
        pltpu.make_async_copy(source.at[pl.ds(first + c * cut, cut)], target.at[pl.ds(c * cut, cut)], sem.at[at + c])
        for c in range(pieces)
    ]


def query_product(x, wq, raw_ref, first, meanwhile):
    rows, depth = x.shape
    size = raw_ref.shape[1]
    cuts = 8
    cut = depth // cuts
    for c in range(cuts):
        a = slice(c * cut, (c + 1) * cut)
        term = mm(x[:, a], wq[a, first : first + size])
        raw_ref[...] = term if c == 0 else raw_ref[...] + term
        meanwhile(c, cuts)


def queries_first_body(x, wq, lam_hbm, prior_hbm, after, raw_ref, lam, prior, acc, sem):
    copies = [pltpu.make_async_copy(lam_hbm, lam, sem.at[0])]
    heads = prior.shape[1]
    for p in range(prior.shape[0]):
        for h in range(heads):
            copies.append(pltpu.make_async_copy(prior_hbm.at[p, h], prior.at[p, h], sem.at[1 + p * heads + h]))
    starts(copies)
    query_product(x, wq, acc, 0, lambda c, cuts: None)
    raw_ref[...] = acc[...]
    for copy in copies:
        copy.wait()


def queries_first(tokens, w_query, level_weights, prior_states, after):
    rows, depth = tokens.shape
    size = w_query.shape[1] // 2
    priors, heads = prior_states.shape[:2]
    return pl.pallas_call(
        queries_first_body,
        in_specs=[VMEM, VMEM, HBM, HBM, ANY],
        out_specs=[VMEM] * 3,
        out_shape=[
            pltpu.VMEM((rows, size), f32),
            pltpu.VMEM(level_weights.shape, f32),
            pltpu.VMEM(prior_states.shape, f32),
        ],
        scratch_shapes=[pltpu.VMEM((rows, size), f32), pltpu.SemaphoreType.DMA((1 + priors * heads,))],
        compiler_params=params(16),
        cost_estimate=cost(2 * rows * depth * size, 2 * (rows * depth + depth * size)),
        name="queries_first",
    )(tokens, w_query, in_hbm(level_weights), in_hbm(prior_states), after)


def queries_second_body(width, x, wq, raw_old, w_hbm, after, qt_ref, raw_ref, w_ref, qt, acc, sem):
    copies = row_copies(w_hbm, 0, w_ref, sem, 0, sem.shape[0])
    starts(copies)
    heads = raw_old.shape[1] // width

    def meanwhile(c, cuts):
        for h in range(c * heads // cuts, (c + 1) * heads // cuts):
            own = slice(h * width, (h + 1) * width)
            leave_tiles(qt, own, finished(raw_old[:, own]))

    query_product(x, wq, acc, raw_old.shape[1], meanwhile)
    raw_ref[...] = acc[...]
    qt_ref[...] = qt[...]
    for copy in copies:
        copy.wait()


def queries_second(tokens, w_query, raw_old, w_out, after, width):
    rows, depth = tokens.shape
    size = w_query.shape[1] // 2
    return pl.pallas_call(
        functools.partial(queries_second_body, width),
        in_specs=[VMEM, VMEM, VMEM, HBM, ANY],
        out_specs=[VMEM] * 3,
        out_shape=[
            pltpu.VMEM((rows // TILE, size, TILE), bf16),
            pltpu.VMEM((rows, size), f32),
            pltpu.VMEM((w_out.shape[0] // 2, w_out.shape[1]), bf16),
        ],
        scratch_shapes=[
            pltpu.VMEM((rows // TILE, size, TILE), bf16),
            pltpu.VMEM((rows, size), f32),
            pltpu.SemaphoreType.DMA((w_out.shape[0] // 32,)),
        ],
        compiler_params=params(16),
        cost_estimate=cost(2 * rows * depth * size, 2 * (rows * depth + depth * size)),
        name="queries_second",
    )(tokens, w_query, raw_old, in_hbm(w_out), after)


def attention_body(width, lam_ref, prior_ref, after, qt_old, raw, k_ref, vt_ref, acc_ref, qt_ref):
    heads = prior_ref.shape[1]
    per = heads // 2
    for h in range(heads):
        own = slice(h % per * width, (h % per + 1) * width)
        every = slice(h * width, (h + 1) * width)
        if h < per:
            qt = whole(qt_old, own)
        else:
            qt = finished(raw[:, own])
            leave_tiles(qt_ref, own, qt)
        prior = [prior_ref[p, h] for p in range(prior_ref.shape[0])]
        pieces = attend(qt, k_ref[:, every], vt_ref[every, :], lam_ref[:, h, :], prior)
        for i, piece in enumerate(pieces):
            acc_ref[i, every, :] = piece


def attention(qt_old, raw, keys, values_t, level_weights, prior_states, after, width):
    tiles, size, take = qt_old.shape
    return pl.pallas_call(
        functools.partial(attention_body, width),
        in_specs=[VMEM] * 2 + [ANY] + [VMEM] * 4,
        out_specs=[VMEM] * 2,
        out_shape=[pltpu.VMEM((tiles, 2 * size, take), f32), pltpu.VMEM(qt_old.shape, bf16)],
        compiler_params=params(16),
        cost_estimate=FAR_APART,
        name="attention",
    )(level_weights, prior_states, after, qt_old, raw, keys, values_t)


def fetch_body(w_hbm, *refs):
    w_ref, sem = refs[-2:]
    copies = row_copies(w_hbm, w_ref.shape[0], w_ref, sem, 0, sem.shape[0])
    starts(copies)
    for copy in copies:
        copy.wait()


def fetch(w_out, after):
    depth, total = w_out.shape
    return pl.pallas_call(
        fetch_body,
        in_specs=[HBM] + [ANY] * len(after),
        out_specs=VMEM,
        out_shape=pltpu.VMEM((depth // 2, total), bf16),
        scratch_shapes=[pltpu.SemaphoreType.DMA((depth // 32,))],
        compiler_params=params(4),
        cost_estimate=cost(0, 2 * depth * total),
        name="fetch",
    )(in_hbm(w_out), *after)


def far_body(width, first_level, halves, counts, first, number, after, *refs):
    refs = list(refs)
    qt_refs = [refs.pop(0) for _ in range(halves)]
    acc_ref = refs.pop(0)
    arrived = [[refs.pop(0) for _ in range(count)] for count in counts]
    lam_ref, gain_ref, out_ref = refs
    nbits = len(counts) // 2
    heads = lam_ref.shape[1]
    half = heads // 2
    per = heads // halves
    mine = lax.axis_index("seq")
    odd = (mine & 1) > 0

    def state(pieces, n):
        each = pieces[0].shape[0]
        return pieces[n // each][n % each]

    for head in range(heads):
        own = slice(head * width, (head + 1) * width)
        states = []
        for j in range(nbits):
            kept, swapped = state(arrived[2 * j], head % half), state(arrived[2 * j + 1], head % half)
            if j == 0:
                states.append(kept if head >= half else swapped)
            else:
                states.append(jnp.where(odd, kept, swapped) if head >= half else jnp.where(odd, swapped, kept))
        states = jnp.concatenate(states, axis=0)
        for i in range(number):
            tile = first + i
            qt = qt_refs[head // per][tile, head % per * width : (head % per + 1) * width, :]
            product = mm(states, qt)
            total = acc_ref[tile, own, :]
            for j in range(nbits):
                lam = lam_ref[first_level + j, head : head + 1, tile * TILE : (tile + 1) * TILE]
                lam = jnp.where(((mine >> j) & 1) > 0, lam, 0.0)
                total = total + lam * product[j * width : (j + 1) * width]
            scale = lax.rsqrt(jnp.mean(total * total, axis=0, keepdims=True) + eps)
            out_ref[i * TILE : (i + 1) * TILE, own] = ((total * scale).T * gain_ref[:, own]).astype(bf16)


def far_part(after, queries_t, acc, states, level_weights, gain, width, first, number):
    levels, heads, rows = level_weights.shape
    total = heads * width
    halves = len(queries_t)
    counts = [len(pieces) for pieces in states]
    states = [piece for pieces in states for piece in pieces]
    return pl.pallas_call(
        functools.partial(far_body, width, rows.bit_length(), halves, counts, first, number),
        in_specs=[ANY] + [VMEM] * (halves + 3 + len(states)),
        out_specs=VMEM,
        out_shape=pltpu.VMEM((number * TILE, total), bf16),
        compiler_params=params(16),
        cost_estimate=cost(8 * rows * width * total, 8 * rows * total),
        name="far_part",
    )(after, *queries_t, acc, *states, level_weights, gain)


def project_body(flip, d, groups, start, take, count, after, w_top, w_low, *refs):
    pieces, added, out_ref = refs[:count], refs[count:-1], refs[-1]
    columns = out_ref.shape[1]
    depth = w_top.shape[0]
    base = lax.rem((lax.axis_index("head") ^ flip) + 2 * d, groups) * columns
    step = min(512, columns)
    for first in range(0, columns, step):
        here = slice(first, first + step)
        there = pl.ds(pl.multiple_of(base + first, 128), step)
        top, low = w_top[:, there], w_low[:, there]
        row = 0
        for a in pieces:
            some = take or a.shape[0]
            total = mm(a[start : start + some, :depth], top) + mm(a[start : start + some, depth:], low)
            for ref in added:
                total = total + ref[start : start + some, here].astype(f32)
            out_ref[row : row + some, here] = total.astype(out_ref.dtype)
            row += some


def project(after, weights, flip, d, groups, pieces, kind, start=0, take=None, added=(), estimate=None):
    depth, columns = weights[0].shape
    columns //= groups
    total = take or sum(a.shape[0] for a in pieces)
    return pl.pallas_call(
        functools.partial(project_body, flip, d, groups, start, take, len(pieces)),
        in_specs=[ANY, VMEM, VMEM] + [VMEM] * (len(pieces) + len(added)),
        out_specs=VMEM,
        out_shape=pltpu.VMEM((total, columns), kind),
        compiler_params=params(16),
        cost_estimate=estimate or cost(4 * total * depth * columns, 4 * depth * columns),
        name="project",
    )(after, *weights, *pieces, *added)


def finish_body(out_in, own_ref, *refs):
    out_ref = refs[-1]
    total = own_ref[...]
    for ref in refs[:-1]:
        total = total + ref[...].astype(f32)
    out_ref[...] = total.astype(bf16)


def finish(out, own, other, terms, first):
    rows, columns = own.shape
    place = lambda i: (first // TILE + i, 0)
    return pl.pallas_call(
        finish_body,
        grid=(terms[0].shape[0] // TILE,),
        in_specs=[ANY] + [pl.BlockSpec((TILE, columns), place)] * 2
        + [pl.BlockSpec((TILE, columns), lambda i: (i, 0))] * len(terms),
        out_specs=pl.BlockSpec((TILE, columns), place),
        out_shape=jax.ShapeDtypeStruct((rows, columns), bf16),
        input_output_aliases={0: 0} if first else {},
        compiler_params=params(16),
        cost_estimate=FAR_APART,
        name="finish",
    )(out, own, other, *terms)


def per_device(tokens, w_query, w_key, w_value, w_out, norm_gain, level_weights, prior_states):
    levels, heads, rows = level_weights.shape
    width = prior_states.shape[-1]
    count = lax.axis_size("seq")
    nbits = count.bit_length() - 1
    groups = lax.axis_size("head")
    chips = groups // 2
    twin = [(i, i ^ 1) for i in range(groups)]
    gain = norm_gain.reshape(1, heads * width)

    def send(state, j):
        return lax.ppermute(state, "seq", [(r, r ^ (1 << j)) for r in range(count)])

    def merge(state, got):
        return (state.astype(f32) + got.astype(f32)).astype(bf16)

    def not_before(value, done):
        return lax.optimization_barrier((value, done))[0]

    tokens, w_query, keys, values_t, keep, give = keys_values(tokens, w_key, w_value, w_query, width)
    got = send(give, 0)
    raw_a, level_weights, prior_states = queries_first(tokens, w_query, level_weights, prior_states, keep)
    got = not_before(got, raw_a)
    running = merge(keep, got)
    kept, swapped = [[got]], []
    for j in range(1, nbits):
        gots = [send(running, j)]
        if j == 1:
            q_a, done, w_top = queries_second(tokens, w_query, raw_a, w_out, running, width)
        if j == nbits - 1:
            acc, q_b = attention(q_a, done, keys, values_t, level_weights, prior_states, running, width)
            swapped = [[send(not_before(keep, running), 0)]] + [[send(not_before(old[0], running), 0)] for old in kept[1:]]
            done = acc
        gots = [not_before(got, done) for got in gots]
        if j < nbits - 1:
            running = merge(running, gots[0])
        kept.append(gots)
    w_low = fetch(w_out, [pieces[0] for pieces in kept[-1:] + swapped])
    swapped.append([not_before(send(got, 0), w_low) for got in kept[-1]])
    states = [pieces for pair in zip(kept, swapped) for pieces in pair]
    queries_t = [q_a, q_b]
    weights = (w_top, w_low)

    def shared(after, piece):
        gots = []
        for d in range(1, chips):
            after = project(after, weights, 1, d, groups, [piece], bf16)
            gots.append(lax.ppermute(after, "head", twin))
        return after, gots

    received = []

    def onward(after, piece, gots, start, take, estimate=None):
        terms = []
        for d in range(1, chips):
            after = project(after, weights, 0, d, groups, [piece], bf16, start, take, gots[d - 1 : d], estimate)
            terms.append(lax.ppermute(after, "head", [(i, (i + 2 * d) % groups) for i in range(groups)]))
        received.append(terms)
        return after

    ahead = far_part(acc, queries_t, acc, states, level_weights, gain, width, 0, 1)
    after, ahead_gots = shared(ahead, ahead)
    rest = far_part(after, queries_t, acc, states, level_weights, gain, width, 1, rows // TILE - 1)
    after = rest
    terms = []
    for d in range(1, chips):
        after = project(after, weights, 0, d, groups, [ahead], f32)
        total = (after + ahead_gots[d - 1].astype(f32)).astype(bf16)
        terms.append(lax.ppermute(total, "head", [(i, (i + 2 * d) % groups) for i in range(groups)]))
    received.append(terms)
    after = total
    after, rest_gots = shared(after, rest)
    after = project(after, weights, 1, 0, groups, [ahead, rest], bf16, estimate=FAR_APART)
    other = lax.ppermute(after, "head", twin)
    after = onward(after, rest, rest_gots, 0, rows - 2 * TILE, FAR_APART)
    after = onward(after, rest, rest_gots, rows - 2 * TILE, TILE)
    own = project(after, weights, 0, 0, groups, [ahead, rest], f32)
    out = finish(gain, own, other, received[0], 0)
    out = finish(out, own, other, received[1], TILE)
    return finish(out, own, other, received[2], rows - TILE)


def solution(mesh):
    placed = (
        P("seq", None),
        P(None, "head"),
        P(None, "head"),
        P(None, "head"),
        P("head", None),
        P("head"),
        P(None, "head", "seq"),
        P(None, "head", None, None),
    )
    return jax.shard_map(
        per_device, mesh=mesh, in_specs=placed, out_specs=P("seq", "head"), check_vma=False
    )
```

```python
import functools

import jax
import jax.numpy as jnp
from jax import lax
from jax.experimental import pallas as pl
from jax.experimental.pallas import tpu as pltpu
from jax.sharding import PartitionSpec as P

eps = 1e-06
TILE = 128
MIB = 1024 * 1024
f32, bf16 = jnp.float32, jnp.bfloat16
HBM = pl.BlockSpec(memory_space=pltpu.HBM)
VMEM = pl.BlockSpec(memory_space=pltpu.VMEM)
SMEM = pl.BlockSpec(memory_space=pltpu.SMEM)
ANY = pl.BlockSpec(memory_space=pl.ANY)


def mm(a, b):
    return jnp.dot(a, b, preferred_element_type=f32)


def params(mib):
    return pltpu.CompilerParams(vmem_limit_bytes=mib * MIB)


def cost(flops, size):
    return pl.CostEstimate(flops=int(flops) // 100, bytes_accessed=int(size) // 100, transcendentals=0)


FAR_APART = pl.CostEstimate(flops=4 * 10**10, bytes_accessed=10**8, transcendentals=0)


def in_hbm(x):
    return pltpu.with_memory_space_constraint(x, pltpu.HBM)


def starts(copies):
    for copy in copies:
        copy.start()


def keys_values_body(
    width, x_hbm, wk_hbm, wv_hbm, wq_hbm, x, wq, k_ref, vt_ref, keep_ref, give_ref, wk, wv, k_acc, v_acc, s, sem
):
    rows, depth = x.shape
    size = wk.shape[1]
    cuts = sem.shape[1]
    cut = depth // cuts
    at = [pl.ds(c * cut, cut) for c in range(cuts)]
    x_in = [pltpu.make_async_copy(x_hbm.at[:, a], x.at[:, a], sem.at[0, c]) for c, a in enumerate(at)]
    v_in = [pltpu.make_async_copy(wv_hbm.at[a], wv.at[a], sem.at[1, c]) for c, a in enumerate(at)]
    k_in = [pltpu.make_async_copy(wk_hbm.at[a], wk.at[a], sem.at[2, c]) for c, a in enumerate(at)]
    q_in = [pltpu.make_async_copy(wq_hbm.at[a], wq.at[a], sem.at[3, c]) for c, a in enumerate(at)]
    for c in range(cuts):
        starts((x_in[c], v_in[c]))
    starts(k_in)
    starts(q_in)
    heads = size // width
    half = heads // 2
    own = [slice(h * width, (h + 1) * width) for h in range(heads)]
    for c, a in enumerate(at):
        x_in[c].wait()
        v_in[c].wait()
        term = mm(x[:, a], wv[a, :])
        v_acc[...] = term if c == 0 else v_acc[...] + term
    for c, a in enumerate(at):
        k_in[c].wait()
        for h in range(c * heads // cuts, (c + 1) * heads // cuts):
            vt_ref[own[h], :] = v_acc[:, own[h]].T.astype(bf16)
        if c == cuts - 1:
            for side in (slice(0, half * width), slice(half * width, size)):
                k_acc[:, side] += mm(x[:, a], wk[a, side])
            continue
        term = mm(x[:, a], wk[a, :])
        k_acc[...] = term if c == 0 else k_acc[...] + term
    for h in range(heads):
        raw = k_acc[:, own[h]]
        key = (raw * lax.rsqrt(jnp.sum(raw * raw, axis=-1, keepdims=True) + eps)).astype(bf16)
        k_ref[:, own[h]] = key
        s[h] = mm(vt_ref[own[h], :], key).astype(bf16)
    first = (lax.axis_index("seq") & 1) * half
    for h in range(half):
        keep_ref[h] = s[first + h]
        give_ref[h] = s[half - first + h]
    for copy in q_in:
        copy.wait()


def keys_values(tokens, w_key, w_value, w_query, width):
    rows, depth = tokens.shape
    size = w_key.shape[1]
    heads = size // width
    cuts = 8
    part = pltpu.VMEM((heads // 2, width, width), bf16)
    return pl.pallas_call(
        functools.partial(keys_values_body, width),
        in_specs=[HBM] * 4,
        out_specs=[VMEM] * 6,
        out_shape=[
            pltpu.VMEM((rows, depth), bf16),
            pltpu.VMEM((depth, size), bf16),
            pltpu.VMEM((rows, size), bf16),
            pltpu.VMEM((size, rows), bf16),
            part,
            part,
        ],
        scratch_shapes=[
            pltpu.VMEM((depth, size), bf16),
            pltpu.VMEM((depth, size), bf16),
            pltpu.VMEM((rows, size), f32),
            pltpu.VMEM((rows, size), f32),
            pltpu.VMEM((heads, width, width), bf16),
            pltpu.SemaphoreType.DMA((4, cuts)),
        ],
        compiler_params=params(30),
        cost_estimate=cost(4 * rows * depth * size, 2 * (rows * depth + 2 * depth * size)),
        name="keys_values",
    )(in_hbm(tokens), in_hbm(w_key), in_hbm(w_value), in_hbm(w_query))


def attend(qt, k, vt, lam, prior):
    width, rows = qt.shape
    shift = rows.bit_length() - 1
    low = TILE.bit_length() - 1
    levels, priors = lam.shape[0], len(prior)
    product = mm(jnp.concatenate([p.astype(bf16).T for p in prior], axis=0), qt)
    total = lam[levels - priors : levels - priors + 1] * product[:width]
    for p in range(1, priors):
        lv = levels - priors + p
        total = total + lam[lv : lv + 1] * product[p * width : (p + 1) * width]
    t_at = lax.broadcasted_iota(jnp.int32, (8, rows), 1) & 7
    s_at = lax.broadcasted_iota(jnp.int32, (8, rows), 0)
    near = jnp.zeros((8, rows), f32)
    for lv in range(4):
        picked = (t_at ^ s_at) >= (1 << lv >> 1)
        near = jnp.where(picked, lam[lv : lv + 1], near)
    near = jnp.where(s_at <= t_at, near, 0.0)
    groups = TILE // 8
    t_group = (lax.broadcasted_iota(jnp.int32, (groups, rows), 1) & (TILE - 1)) >> 3
    s_group = lax.broadcasted_iota(jnp.int32, (groups, rows), 0)
    wide = jnp.zeros((groups, rows), f32)
    for lv in range(4, low + 1):
        picked = (t_group ^ s_group) >= (1 << (lv - 4))
        wide = jnp.where(picked, lam[lv : lv + 1], wide)
    wide = jnp.where(s_group < t_group, wide, 0.0)
    lane_group = (lax.broadcasted_iota(jnp.int32, (8, TILE), 1)) >> 3
    pieces = []
    for i in range(rows // TILE):
        here = slice(i * TILE, (i + 1) * TILE)
        scores = mm(k[here], qt[:, here])
        mixing = []
        for g in range(groups):
            weight = jnp.where(lane_group == g, near[:, here], wide[g : g + 1, here])
            mixing.append(weight * scores[g * 8 : g * 8 + 8])
        mixing = jnp.concatenate(mixing, axis=0).astype(bf16)
        pieces.append(total[:, here] + mm(vt[:, here], mixing))
    for bit in range(low, shift):
        half = 1 << bit
        for start in range(half, rows, 2 * half):
            past = slice(start - half, start)
            here = slice(start, start + half)
            state = mm(vt[:, past], k[past]).astype(bf16)
            found = lam[1 + bit : 2 + bit, here] * mm(state, qt[:, here])
            for n in range(half // TILE):
                i = start // TILE + n
                pieces[i] = pieces[i] + found[:, n * TILE : (n + 1) * TILE]
    return pieces


def whole(qt_ref, at):
    return jnp.concatenate([qt_ref[i, at, :] for i in range(qt_ref.shape[0])], axis=1)


def finished(raw):
    raw = raw.T
    return (raw * lax.rsqrt(jnp.sum(raw * raw, axis=0, keepdims=True) + eps)).astype(bf16)


def leave_tiles(ref, at, qt):
    for i in range(ref.shape[0]):
        ref[i, at, :] = qt[:, i * TILE : (i + 1) * TILE]


def row_copies(source, first, target, sem, at, pieces):
    cut = target.shape[0] // pieces
    return [
        pltpu.make_async_copy(source.at[pl.ds(first + c * cut, cut)], target.at[pl.ds(c * cut, cut)], sem.at[at + c])
        for c in range(pieces)
    ]


def query_product(x, wq, raw_ref, first, meanwhile):
    rows, depth = x.shape
    size = raw_ref.shape[1]
    cuts = 8
    cut = depth // cuts
    for c in range(cuts):
        a = slice(c * cut, (c + 1) * cut)
        term = mm(x[:, a], wq[a, first : first + size])
        raw_ref[...] = term if c == 0 else raw_ref[...] + term
        meanwhile(c, cuts)


def queries_first_body(x, wq, lam_hbm, prior_hbm, after, raw_ref, lam, prior, acc, sem):
    copies = [pltpu.make_async_copy(lam_hbm, lam, sem.at[0])]
    heads = prior.shape[1]
    for p in range(prior.shape[0]):
        for h in range(heads):
            copies.append(pltpu.make_async_copy(prior_hbm.at[p, h], prior.at[p, h], sem.at[1 + p * heads + h]))
    starts(copies)
    query_product(x, wq, acc, 0, lambda c, cuts: None)
    raw_ref[...] = acc[...]
    for copy in copies:
        copy.wait()


def queries_first(tokens, w_query, level_weights, prior_states, after):
    rows, depth = tokens.shape
    size = w_query.shape[1] // 2
    priors, heads = prior_states.shape[:2]
    return pl.pallas_call(
        queries_first_body,
        in_specs=[VMEM, VMEM, HBM, HBM, ANY],
        out_specs=[VMEM] * 3,
        out_shape=[
            pltpu.VMEM((rows, size), f32),
            pltpu.VMEM(level_weights.shape, f32),
            pltpu.VMEM(prior_states.shape, f32),
        ],
        scratch_shapes=[pltpu.VMEM((rows, size), f32), pltpu.SemaphoreType.DMA((1 + priors * heads,))],
        compiler_params=params(16),
        cost_estimate=cost(2 * rows * depth * size, 2 * (rows * depth + depth * size)),
        name="queries_first",
    )(tokens, w_query, in_hbm(level_weights), in_hbm(prior_states), after)


def queries_second_body(width, x, wq, raw_old, w_hbm, after, qt_ref, raw_ref, w_ref, qt, acc, sem):
    copies = row_copies(w_hbm, 0, w_ref, sem, 0, sem.shape[0])
    starts(copies)
    heads = raw_old.shape[1] // width

    def meanwhile(c, cuts):
        for h in range(c * heads // cuts, (c + 1) * heads // cuts):
            own = slice(h * width, (h + 1) * width)
            leave_tiles(qt, own, finished(raw_old[:, own]))

    query_product(x, wq, acc, raw_old.shape[1], meanwhile)
    raw_ref[...] = acc[...]
    qt_ref[...] = qt[...]
    for copy in copies:
        copy.wait()


def queries_second(tokens, w_query, raw_old, w_out, after, width):
    rows, depth = tokens.shape
    size = w_query.shape[1] // 2
    return pl.pallas_call(
        functools.partial(queries_second_body, width),
        in_specs=[VMEM, VMEM, VMEM, HBM, ANY],
        out_specs=[VMEM] * 3,
        out_shape=[
            pltpu.VMEM((rows // TILE, size, TILE), bf16),
            pltpu.VMEM((rows, size), f32),
            pltpu.VMEM((w_out.shape[0] // 2, w_out.shape[1]), bf16),
        ],
        scratch_shapes=[
            pltpu.VMEM((rows // TILE, size, TILE), bf16),
            pltpu.VMEM((rows, size), f32),
            pltpu.SemaphoreType.DMA((w_out.shape[0] // 32,)),
        ],
        compiler_params=params(16),
        cost_estimate=cost(2 * rows * depth * size, 2 * (rows * depth + depth * size)),
        name="queries_second",
    )(tokens, w_query, raw_old, in_hbm(w_out), after)


def attention_body(width, lam_ref, prior_ref, after, qt_old, raw, k_ref, vt_ref, acc_ref, qt_ref):
    heads = prior_ref.shape[1]
    per = heads // 2
    for h in range(heads):
        own = slice(h % per * width, (h % per + 1) * width)
        every = slice(h * width, (h + 1) * width)
        if h < per:
            qt = whole(qt_old, own)
        else:
            qt = finished(raw[:, own])
            leave_tiles(qt_ref, own, qt)
        prior = [prior_ref[p, h] for p in range(prior_ref.shape[0])]
        pieces = attend(qt, k_ref[:, every], vt_ref[every, :], lam_ref[:, h, :], prior)
        for i, piece in enumerate(pieces):
            acc_ref[i, every, :] = piece


def attention(qt_old, raw, keys, values_t, level_weights, prior_states, after, width):
    tiles, size, take = qt_old.shape
    return pl.pallas_call(
        functools.partial(attention_body, width),
        in_specs=[VMEM] * 2 + [ANY] + [VMEM] * 4,
        out_specs=[VMEM] * 2,
        out_shape=[pltpu.VMEM((tiles, 2 * size, take), f32), pltpu.VMEM(qt_old.shape, bf16)],
        compiler_params=params(16),
        cost_estimate=FAR_APART,
        name="attention",
    )(level_weights, prior_states, after, qt_old, raw, keys, values_t)


def fetch_body(w_hbm, *refs):
    w_ref, sem = refs[-2:]
    copies = row_copies(w_hbm, w_ref.shape[0], w_ref, sem, 0, sem.shape[0])
    starts(copies)
    for copy in copies:
        copy.wait()


def fetch(w_out, after):
    depth, total = w_out.shape
    return pl.pallas_call(
        fetch_body,
        in_specs=[HBM] + [ANY] * len(after),
        out_specs=VMEM,
        out_shape=pltpu.VMEM((depth // 2, total), bf16),
        scratch_shapes=[pltpu.SemaphoreType.DMA((depth // 32,))],
        compiler_params=params(4),
        cost_estimate=cost(0, 2 * depth * total),
        name="fetch",
    )(in_hbm(w_out), *after)


def far_body(width, first_level, halves, counts, first, number, after, *refs):
    refs = list(refs)
    qt_refs = [refs.pop(0) for _ in range(halves)]
    acc_ref = refs.pop(0)
    arrived = [[refs.pop(0) for _ in range(count)] for count in counts]
    lam_ref, gain_ref, out_ref = refs
    nbits = len(counts) // 2
    heads = lam_ref.shape[1]
    half = heads // 2
    per = heads // halves
    mine = lax.axis_index("seq")
    odd = (mine & 1) > 0

    def state(pieces, n):
        each = pieces[0].shape[0]
        return pieces[n // each][n % each]

    for head in range(heads):
        own = slice(head * width, (head + 1) * width)
        states = []
        for j in range(nbits):
            kept, swapped = state(arrived[2 * j], head % half), state(arrived[2 * j + 1], head % half)
            if j == 0:
                states.append(kept if head >= half else swapped)
            else:
                states.append(jnp.where(odd, kept, swapped) if head >= half else jnp.where(odd, swapped, kept))
        states = jnp.concatenate(states, axis=0)
        for i in range(number):
            tile = first + i
            qt = qt_refs[head // per][tile, head % per * width : (head % per + 1) * width, :]
            product = mm(states, qt)
            total = acc_ref[tile, own, :]
            for j in range(nbits):
                lam = lam_ref[first_level + j, head : head + 1, tile * TILE : (tile + 1) * TILE]
                lam = jnp.where(((mine >> j) & 1) > 0, lam, 0.0)
                total = total + lam * product[j * width : (j + 1) * width]
            scale = lax.rsqrt(jnp.mean(total * total, axis=0, keepdims=True) + eps)
            out_ref[i * TILE : (i + 1) * TILE, own] = ((total * scale).T * gain_ref[:, own]).astype(bf16)


def far_part(after, queries_t, acc, states, level_weights, gain, width, first, number):
    levels, heads, rows = level_weights.shape
    total = heads * width
    halves = len(queries_t)
    counts = [len(pieces) for pieces in states]
    states = [piece for pieces in states for piece in pieces]
    return pl.pallas_call(
        functools.partial(far_body, width, rows.bit_length(), halves, counts, first, number),
        in_specs=[ANY] + [VMEM] * (halves + 3 + len(states)),
        out_specs=VMEM,
        out_shape=pltpu.VMEM((number * TILE, total), bf16),
        compiler_params=params(16),
        cost_estimate=cost(8 * rows * width * total, 8 * rows * total),
        name="far_part",
    )(after, *queries_t, acc, *states, level_weights, gain)


def project_body(flip, d, groups, start, take, count, after, w_top, w_low, *refs):
    pieces, added, out_ref = refs[:count], refs[count:-1], refs[-1]
    columns = out_ref.shape[1]
    depth = w_top.shape[0]
    base = lax.rem((lax.axis_index("head") ^ flip) + 2 * d, groups) * columns
    step = min(512, columns)
    for first in range(0, columns, step):
        here = slice(first, first + step)
        there = pl.ds(pl.multiple_of(base + first, 128), step)
        top, low = w_top[:, there], w_low[:, there]
        row = 0
        for a in pieces:
            some = take or a.shape[0]
            total = mm(a[start : start + some, :depth], top) + mm(a[start : start + some, depth:], low)
            for ref in added:
                total = total + ref[start : start + some, here].astype(f32)
            out_ref[row : row + some, here] = total.astype(out_ref.dtype)
            row += some


def project(after, weights, flip, d, groups, pieces, kind, start=0, take=None, added=(), estimate=None):
    depth, columns = weights[0].shape
    columns //= groups
    total = take or sum(a.shape[0] for a in pieces)
    return pl.pallas_call(
        functools.partial(project_body, flip, d, groups, start, take, len(pieces)),
        in_specs=[ANY, VMEM, VMEM] + [VMEM] * (len(pieces) + len(added)),
        out_specs=VMEM,
        out_shape=pltpu.VMEM((total, columns), kind),
        compiler_params=params(16),
        cost_estimate=estimate or cost(4 * total * depth * columns, 4 * depth * columns),
        name="project",
    )(after, *weights, *pieces, *added)


def finish_body(out_in, own_ref, *refs):
    out_ref = refs[-1]
    total = own_ref[...]
    for ref in refs[:-1]:
        total = total + ref[...].astype(f32)
    out_ref[...] = total.astype(bf16)


def finish(out, own, other, terms, first):
    rows, columns = own.shape
    place = lambda i: (first // TILE + i, 0)
    return pl.pallas_call(
        finish_body,
        grid=(terms[0].shape[0] // TILE,),
        in_specs=[ANY] + [pl.BlockSpec((TILE, columns), place)] * 2
        + [pl.BlockSpec((TILE, columns), lambda i: (i, 0))] * len(terms),
        out_specs=pl.BlockSpec((TILE, columns), place),
        out_shape=jax.ShapeDtypeStruct((rows, columns), bf16),
        input_output_aliases={0: 0} if first else {},
        compiler_params=params(16),
        cost_estimate=FAR_APART,
        name="finish",
    )(out, own, other, *terms)


def per_device(tokens, w_query, w_key, w_value, w_out, norm_gain, level_weights, prior_states):
    levels, heads, rows = level_weights.shape
    width = prior_states.shape[-1]
    count = lax.axis_size("seq")
    nbits = count.bit_length() - 1
    groups = lax.axis_size("head")
    chips = groups // 2
    twin = [(i, i ^ 1) for i in range(groups)]
    gain = norm_gain.reshape(1, heads * width)

    def send(state, j):
        return lax.ppermute(state, "seq", [(r, r ^ (1 << j)) for r in range(count)])

    def merge(state, got):
        return (state.astype(f32) + got.astype(f32)).astype(bf16)

    def not_before(value, done):
        return lax.optimization_barrier((value, done))[0]

    tokens, w_query, keys, values_t, keep, give = keys_values(tokens, w_key, w_value, w_query, width)
    got = send(give, 0)
    raw_a, level_weights, prior_states = queries_first(tokens, w_query, level_weights, prior_states, keep)
    got = not_before(got, raw_a)
    running = merge(keep, got)
    kept, swapped = [[got]], []
    for j in range(1, nbits):
        gots = [send(running, j)]
        if j == 1:
            q_a, done, w_top = queries_second(tokens, w_query, raw_a, w_out, running, width)
        if j == nbits - 1:
            acc, q_b = attention(q_a, done, keys, values_t, level_weights, prior_states, running, width)
            swapped = [[send(not_before(keep, running), 0)]] + [[send(not_before(old[0], running), 0)] for old in kept[1:]]
            done = acc
        gots = [not_before(got, done) for got in gots]
        if j < nbits - 1:
            running = merge(running, gots[0])
        kept.append(gots)
    w_low = fetch(w_out, [pieces[0] for pieces in kept[-1:] + swapped])
    swapped.append([not_before(send(got, 0), w_low) for got in kept[-1]])
    states = [pieces for pair in zip(kept, swapped) for pieces in pair]
    queries_t = [q_a, q_b]
    weights = (w_top, w_low)

    def shared(after, piece):
        gots = []
        for d in range(1, chips):
            after = project(after, weights, 1, d, groups, [piece], bf16)
            gots.append(lax.ppermute(after, "head", twin))
        return after, gots

    received = []

    def onward(after, piece, gots, start, take, estimate=None):
        terms = []
        for d in range(1, chips):
            after = project(after, weights, 0, d, groups, [piece], bf16, start, take, gots[d - 1 : d], estimate)
            terms.append(lax.ppermute(after, "head", [(i, (i + 2 * d) % groups) for i in range(groups)]))
        received.append(terms)
        return after

    ahead = far_part(acc, queries_t, acc, states, level_weights, gain, width, 0, 1)
    after, ahead_gots = shared(ahead, ahead)
    rest = far_part(after, queries_t, acc, states, level_weights, gain, width, 1, rows // TILE - 1)
    after = rest
    terms = []
    for d in range(1, chips):
        after = project(after, weights, 0, d, groups, [ahead], f32)
        total = (after + ahead_gots[d - 1].astype(f32)).astype(bf16)
        terms.append(lax.ppermute(total, "head", [(i, (i + 2 * d) % groups) for i in range(groups)]))
    received.append(terms)
    after = total
    after, rest_gots = shared(after, rest)
    after = project(after, weights, 1, 0, groups, [ahead, rest], bf16, estimate=FAR_APART)
    other = lax.ppermute(after, "head", twin)
    after = onward(after, rest, rest_gots, 0, rows - 2 * TILE, FAR_APART)
    after = onward(after, rest, rest_gots, rows - 2 * TILE, TILE)
    own = project(after, weights, 0, 0, groups, [ahead, rest], f32)
    out = finish(gain, own, other, received[0], 0)
    out = finish(out, own, other, received[1], TILE)
    return finish(out, own, other, received[2], rows - TILE)


def solution(mesh):
    placed = (
        P("seq", None),
        P(None, "head"),
        P(None, "head"),
        P(None, "head"),
        P("head", None),
        P("head"),
        P(None, "head", "seq"),
        P(None, "head", None, None),
    )
    return jax.shard_map(
        per_device, mesh=mesh, in_specs=placed, out_specs=P("seq", "head"), check_vma=False
    )
```
